32 devices in a mesh: section: 2 (over x), shard: 4 (over z), replica: 4 (over y, core).
Axes of the slice: x: 2, y: 2, z: 4, core: 2. Of those that a mesh axis runs over, the one named last changes fastest.
Arguments:
- tokens: bfloat16 [16384, 768], P(('shard', 'replica')), may hold values from -6 to 6
- cotangent: bfloat16 [16384, 768], P(('shard', 'replica')), may hold values from -6 to 6
- lengths: int32 [32, 4], replicated, may hold values from 0 to 512, as said below
- assignment: int32 [32], replicated, may hold values from 0 to 31, each once
- attention_gain: bfloat16 [2, 768], P('section', 'shard'), may hold values from 0.25 to 1.75
- attention_shift: bfloat16 [2, 768], P('section', 'shard'), may hold values from -2 to 2
- input_weight: bfloat16 [2, 768, 2304], P('section', 'shard'), may hold values from -0.21875 to 0.21875
- query_bias: bfloat16 [2, 768], P('section', 'shard'), may hold values from -2 to 2
- value_bias: bfloat16 [2, 768], P('section', 'shard'), may hold values from -2 to 2
- output_weight: bfloat16 [2, 768, 768], P('section', 'shard'), may hold values from -0.625 to 0.625
- output_bias: bfloat16 [2, 768], P('section', 'shard'), may hold values from -2 to 2
- feedforward_gain: bfloat16 [2, 768], P('section', 'shard'), may hold values from 0.25 to 1.75
- feedforward_shift: bfloat16 [2, 768], P('section', 'shard'), may hold values from -2 to 2
- expand_weight: bfloat16 [2, 768, 3072], P('section', 'shard'), may hold values from -0.21875 to 0.21875
- expand_bias: bfloat16 [2, 3072], P('section', 'shard'), may hold values from -2 to 2
- contract_weight: bfloat16 [2, 3072, 768], P('section', 'shard'), may hold values from -0.15625 to 0.15625
- contract_bias: bfloat16 [2, 768], P('section', 'shard'), may hold values from -2 to 2
Outputs:
- block_outputs: bfloat16 [2, 16384, 768], P('section', ('shard', 'replica'))
- input_grads: float32 [2, 16384, 768], P('section', ('shard', 'replica'))
- attention_gain_gradient: float32 [2, 768], P('section', 'shard')
- attention_shift_gradient: float32 [2, 768], P('section', 'shard')
- input_weight_gradient: float32 [2, 768, 2304], P('section', 'shard')
- query_bias_gradient: float32 [2, 768], P('section', 'shard')
- value_bias_gradient: float32 [2, 768], P('section', 'shard')
- output_weight_gradient: float32 [2, 768, 768], P('section', 'shard')
- output_bias_gradient: float32 [2, 768], P('section', 'shard')
- feedforward_gain_gradient: float32 [2, 768], P('section', 'shard')
- feedforward_shift_gradient: float32 [2, 768], P('section', 'shard')
- expand_weight_gradient: float32 [2, 768, 3072], P('section', 'shard')
- expand_bias_gradient: float32 [2, 3072], P('section', 'shard')
- contract_weight_gradient: float32 [2, 3072, 768], P('section', 'shard')
- contract_bias_gradient: float32 [2, 768], P('section', 'shard')
The draws below stay inside these ranges and needn't reach their ends.
Inputs may be any that keep to these rules, and one draw needn't show every extreme that they name: `lengths`: row g lists the token counts of group g's 4 sequences in order, zero for an empty entry; each row sums to at most 512, and some row holds a single sequence of 512 tokens. `assignment`: every slot receives exactly one group.
All inputs are finite; a program needn't handle non-finite values.
Results may differ from the reference program's by a relative error of at most 0.022.
Values may be sent and summed in bfloat16 or wider, within the bound.
No kernel may reach another device: no remote copies, remote signals or barrier semaphores. Data moves between devices by JAX's collectives and lax.ppermute only.
A program may use at most 448 MiB of HBM per device.

```python
import jax
import jax.numpy as jnp
from jax import lax

D = 768
HEADS = 12
FF = 3072
ROWS = 512
SEQ_SLOT = 4
SLOTS = 32
TOKENS = 16384


def draw_lengths(key, part):
    key = jax.random.fold_in(key, 11)
    total_key, cut_key, whole_key = jax.random.split(key, 3)
    totals = jax.random.randint(total_key, (SLOTS,), ROWS // 8, ROWS + 1, dtype=jnp.int32)
    cut_points = jnp.sort(jax.random.randint(cut_key, (SLOTS, SEQ_SLOT - 1), 0, ROWS + 1, dtype=jnp.int32), axis=1)
    cut_points = cut_points * totals[:, None] // ROWS
    edge_points = jnp.concatenate([jnp.zeros((SLOTS, 1), jnp.int32), cut_points, totals[:, None]], axis=1)
    counts = edge_points[:, 1:] - edge_points[:, :-1]
    chosen = jax.random.randint(whole_key, (), 0, SLOTS, dtype=jnp.int32)
    single = jnp.zeros((SEQ_SLOT,), jnp.int32).at[0].set(ROWS)
    row_numbers = jnp.arange(SLOTS, dtype=jnp.int32)
    return jnp.where((row_numbers == chosen)[:, None], single[None, :], counts).astype(jnp.int32)


def block_levels(own_key, extent, cuts, least, largest):
    loudness, own = 1.0, jax.random.fold_in(own_key, 6)
    for position, shards_of in cuts:
        draws = jnp.exp(jax.random.uniform(jax.random.fold_in(own, position), (shards_of,), jnp.float32, least / len(cuts), largest / len(cuts)))
        loudness = loudness * jnp.repeat(draws, extent[position] // shards_of).reshape([-1 if axis == position else 1 for axis in range(len(extent))])
    return loudness


def scatter_about(own_key, shape, scale, most, shards=(), held_as=jnp.bfloat16):
    level = block_levels(own_key, shape, shards, -0.22, 0.18) if shards else 1.0
    array = jax.random.normal(own_key, shape, jnp.float32) * scale * level
    return jnp.minimum(jnp.maximum(array, -most), most).astype(held_as)


def setup_inputs(seed: int = 0) -> dict:
    key_of = jax.random.split(jax.random.key(seed), 18)
    tokens = scatter_about(key_of[0], (TOKENS, D), 1.0, 6.0, ((0, 16),))
    cotangent = scatter_about(key_of[1], (TOKENS, D), 1.0, 6.0, ((0, 16),))
    lengths = draw_lengths(jax.random.fold_in(key_of[17], 71), 0)
    assignment = jax.random.permutation(key_of[3], SLOTS).astype(jnp.int32)
    attention_gain = jnp.clip(1.0 + 0.15 * jax.random.normal(key_of[4], (2, D), jnp.float32), 0.25, 1.75).astype(jnp.bfloat16)
    attention_shift = scatter_about(key_of[5], (2, D), 0.3, 2.0, ((0, 2), (1, 4)))
    input_weight = scatter_about(key_of[6], (2, D, 3 * D), D ** -0.5, 0.21875, ((0, 2), (1, 4)))
    query_bias = scatter_about(key_of[7], (2, D), 0.3, 2.0, ((0, 2), (1, 4)))
    value_bias = scatter_about(key_of[8], (2, D), 0.3, 2.0, ((0, 2), (1, 4)))
    output_weight = scatter_about(key_of[9], (2, D, D), (D // 8) ** -0.5, 0.625, ((0, 2), (1, 4)))
    output_bias = scatter_about(key_of[10], (2, D), 0.3, 2.0, ((0, 2), (1, 4)))
    feedforward_gain = jnp.clip(1.0 + 0.15 * jax.random.normal(key_of[11], (2, D), jnp.float32), 0.25, 1.75).astype(jnp.bfloat16)
    feedforward_shift = scatter_about(key_of[12], (2, D), 0.3, 2.0, ((0, 2), (1, 4)))
    expand_weight = scatter_about(key_of[13], (2, D, FF), D ** -0.5, 0.21875, ((0, 2), (1, 4)))
    expand_bias = scatter_about(key_of[14], (2, FF), 0.3, 2.0, ((0, 2), (1, 4)))
    contract_weight = scatter_about(key_of[15], (2, FF, D), (FF // 2) ** -0.5, 0.15625, ((0, 2), (1, 4)))
    contract_bias = scatter_about(key_of[16], (2, D), 0.3, 2.0, ((0, 2), (1, 4)))
    return dict(tokens=tokens, cotangent=cotangent, lengths=lengths, assignment=assignment, attention_gain=attention_gain, attention_shift=attention_shift, input_weight=input_weight, query_bias=query_bias, value_bias=value_bias, output_weight=output_weight, output_bias=output_bias, feedforward_gain=feedforward_gain, feedforward_shift=feedforward_shift, expand_weight=expand_weight, expand_bias=expand_bias, contract_weight=contract_weight, contract_bias=contract_bias)


EPSILON = 1e-05
MASKED_SCORE = -1e+30
EXACT = lax.Precision.HIGHEST

@jax.custom_vjp
def low(v):
    return lax.optimization_barrier(v.astype(jnp.bfloat16)).astype(jnp.float32)

@jax.custom_vjp
def low_back(v):
    return v

def low_keep(v):
    return (low(v), None)

def low_pass(kept, grad):
    return (grad,)

def back_keep(v):
    return (v, None)

def back_low(kept, grad):
    return (low(grad),)
low.defvjp(low_keep, low_pass)
low_back.defvjp(back_keep, back_low)

def layer_norm(hidden, norm_gain, norm_shift):
    center = hidden - lax.optimization_barrier(jnp.mean(hidden, axis=-1, keepdims=True))
    spread = lax.optimization_barrier(jnp.mean(center * center, axis=-1, keepdims=True))
    return center * lax.rsqrt(spread + EPSILON) * norm_gain + norm_shift

def slot_layout(counts, row_count):
    bounds = jnp.cumsum(counts, dtype=jnp.int32)
    places = jnp.arange(row_count, dtype=jnp.int32)
    segment = lax.optimization_barrier(jnp.sum((bounds[None, :] <= places[:, None]).astype(jnp.int32), axis=1, dtype=jnp.int32))
    living = (places < bounds[-1]).astype(jnp.float32)
    return (segment, living)

def block_exact(params, hidden, segment, living):
    attention_gain, attention_shift, input_weight, query_bias, value_bias, output_weight, output_bias, feedforward_gain, feedforward_shift, expand_weight, expand_bias, contract_weight, contract_bias = params
    row_count, model_width = hidden.shape
    head_dim = model_width // HEADS
    normed = low(layer_norm(hidden, attention_gain, attention_shift))
    joint_bias = jnp.concatenate([query_bias, jnp.zeros_like(query_bias), value_bias])
    joint = low(low_back(jnp.dot(normed, input_weight, precision=EXACT) + joint_bias))
    shaped = joint.reshape(row_count, 3, HEADS, head_dim)
    queries = shaped[:, 0]
    keys_all = shaped[:, 1]
    values = shaped[:, 2]
    scores = jnp.einsum('qhd,khd->hqk', queries, keys_all, precision=EXACT) * head_dim ** (-0.5)
    scores = low_back(scores)
    places = jnp.arange(row_count, dtype=jnp.int32)
    allowed = (segment[:, None] == segment[None, :]) & (places[None, :] <= places[:, None])
    scores = jnp.where(allowed[None], scores, MASKED_SCORE)
    row_max = lax.optimization_barrier(jnp.max(scores, axis=-1, keepdims=True))
    exponent = jnp.exp(scores - row_max)
    probabilities = low(exponent / lax.optimization_barrier(jnp.sum(exponent, axis=-1, keepdims=True)))
    mixed = jnp.einsum('hqk,khd->qhd', probabilities, values, precision=EXACT).reshape(row_count, model_width)
    mixed = low(low_back(mixed))
    branch = low_back(jnp.dot(mixed, output_weight, precision=EXACT) + output_bias)
    middle = hidden + branch
    normed_two = low(layer_norm(middle, feedforward_gain, feedforward_shift))
    expanded = low_back(jnp.dot(normed_two, expand_weight, precision=EXACT) + expand_bias)
    activated = low(jax.nn.gelu(expanded, approximate=True))
    contracted = low_back(jnp.dot(activated, contract_weight, precision=EXACT) + contract_bias)
    return (middle + contracted) * living[:, None]

def reference(tokens, cotangent, lengths, assignment, attention_gain, attention_shift, input_weight, query_bias, value_bias, output_weight, output_bias, feedforward_gain, feedforward_shift, expand_weight, expand_bias, contract_weight, contract_bias):
    params = tuple((member.astype(jnp.float32) for member in (attention_gain, attention_shift, input_weight, query_bias, value_bias, output_weight, output_bias, feedforward_gain, feedforward_shift, expand_weight, expand_bias, contract_weight, contract_bias)))
    model_width = tokens.shape[1]
    slot_owner = jnp.zeros((SLOTS,), jnp.int32).at[assignment].set(jnp.arange(SLOTS, dtype=jnp.int32))
    slot_counts = lengths[slot_owner]
    segments, livings = jax.vmap(lambda counts: slot_layout(counts, ROWS))(slot_counts)
    inputs = tokens.astype(jnp.float32).reshape(SLOTS, ROWS, model_width)
    seeds = cotangent.astype(jnp.float32).reshape(SLOTS, ROWS, model_width)
    offsets = jnp.zeros_like(inputs)

    def whole(params_all, first_inputs, offset_all):

        def one_slot(state_value, slot_inputs):
            first_in, offset_in, segment, living = slot_inputs
            first_params = tuple((member[0] for member in params_all))
            second_params = tuple((member[1] for member in params_all))
            first_out = block_exact(first_params, first_in, segment, living)
            second_in = low(low_back(first_out)) + offset_in
            second_out = block_exact(second_params, second_in, segment, living)
            return (state_value, (second_out, first_out))
        _, (second_out, first_out) = lax.scan(jax.checkpoint(one_slot), jnp.zeros((), jnp.float32), (first_inputs, offset_all, segments, livings))
        return (second_out, first_out)
    second_out, pullback, first_out = jax.vjp(whole, params, inputs, offsets, has_aux=True)
    param_grads, first_grad, second_grad = pullback(seeds)
    block_outputs = jnp.stack([first_out, second_out]).reshape(2, TOKENS, model_width).astype(jnp.bfloat16)
    input_grads = jnp.stack([first_grad, second_grad]).reshape(2, TOKENS, model_width)
    return (block_outputs, input_grads, param_grads[0], param_grads[1], param_grads[2], param_grads[3], param_grads[4], param_grads[5], param_grads[6], param_grads[7], param_grads[8], param_grads[9], param_grads[10], param_grads[11], param_grads[12])
```

```python
import jax
import jax.numpy as jnp
from jax import lax
from jax.experimental import pallas as pl
from jax.experimental.pallas import tpu as pltpu
from jax.sharding import PartitionSpec as P

HEADS = 12
ROWS = 512
MICRO = 2


EPSILON = 1e-05
MASKED_SCORE = -1e30


def layer_norm(hidden, norm_gain, norm_shift):
    center = hidden - jnp.mean(hidden, axis=-1, keepdims=True)
    spread = jnp.mean(center * center, axis=-1, keepdims=True)
    return center * lax.rsqrt(spread + EPSILON) * norm_gain + norm_shift


def slot_layout(counts, row_count):
    bounds = jnp.cumsum(counts, dtype=jnp.int32)
    places = jnp.arange(row_count, dtype=jnp.int32)
    segment = jnp.sum(
        (bounds[None, :] <= places[:, None]).astype(jnp.int32), axis=1, dtype=jnp.int32
    )
    living = (places < bounds[-1]).astype(jnp.float32)
    return (segment, living)


def gelu_tanh(values):
    return jax.nn.gelu(values, approximate=True)


def contract_rows(left_side, right_side):
    return lax.dot_general(
        left_side, right_side, (((0,), (0,)), ((), ())), preferred_element_type=jnp.float32
    )


def times_transpose(left_side, right_side):
    return lax.dot_general(
        left_side, right_side, (((1,), (1,)), ((), ())), preferred_element_type=jnp.float32
    )


def split_heads(joint_low):
    row_count, three_width = joint_low.shape
    model_width = three_width // 3
    shaped = joint_low.reshape(row_count, 3, HEADS, model_width // HEADS)
    return (shaped[:, 0], shaped[:, 1], shaped[:, 2])


def masked_scores(block_queries, keys_all, segment, first_row, score_scale):
    block_count = block_queries.shape[0]
    scores = (
        jnp.einsum("qhd,khd->hqk", block_queries, keys_all, preferred_element_type=jnp.float32)
        * score_scale
    )
    query_places = first_row + jnp.arange(block_count, dtype=jnp.int32)
    key_places = jnp.arange(keys_all.shape[0], dtype=jnp.int32)
    same_segment = segment[first_row : first_row + block_count, None] == segment[None, :]
    allowed = same_segment & (key_places[None, :] <= query_places[:, None])
    return jnp.where(allowed[None], scores, MASKED_SCORE)


def attend_forward(joint_low, segment):
    queries, keys_all, values = split_heads(joint_low)
    row_count, head_count, head_dim = queries.shape
    score_scale = head_dim ** (-0.5)
    scores = masked_scores(queries, keys_all, segment, 0, score_scale)
    row_max = jnp.max(scores, axis=-1, keepdims=True)
    exponent = jnp.exp(scores - row_max)
    row_total = jnp.sum(exponent, axis=-1, keepdims=True)
    probabilities = (exponent / row_total).astype(jnp.bfloat16)
    outputs = [
        jnp.einsum("hqk,khd->qhd", probabilities, values, preferred_element_type=jnp.float32)
    ]
    log_parts = [(row_max + jnp.log(row_total))[:, :, 0]]
    mixed = jnp.concatenate(outputs, axis=0).reshape(row_count, head_count * head_dim)
    return (mixed, jnp.concatenate(log_parts, axis=1))


def attend_backward(joint_low, log_sums, mixed_grad, segment):
    queries, keys_all, values = split_heads(joint_low)
    row_count, head_count, head_dim = queries.shape
    model_width = head_count * head_dim
    score_scale = head_dim ** (-0.5)
    block_rows = min(512, row_count)
    grad_heads = mixed_grad.reshape(row_count, head_count, head_dim)
    key_grad = jnp.zeros((row_count, head_count, head_dim), jnp.float32)
    value_grad = jnp.zeros((row_count, head_count, head_dim), jnp.float32)
    scores = masked_scores(queries, keys_all, segment, 0, score_scale)
    probabilities = jnp.exp(scores - log_sums[:, 0:block_rows, None])
    probs_low = probabilities.astype(jnp.bfloat16)
    value_grad = value_grad + jnp.einsum(
        "hqk,qhd->khd", probs_low, grad_heads, preferred_element_type=jnp.float32
    )
    prob_grad = jnp.einsum("qhd,khd->hqk", grad_heads, values, preferred_element_type=jnp.float32)
    centered = prob_grad - jnp.sum(prob_grad * probabilities, axis=-1, keepdims=True)
    score_grad = (probabilities * centered).astype(jnp.bfloat16)
    query_parts = [
        jnp.einsum("hqk,khd->qhd", score_grad, keys_all, preferred_element_type=jnp.float32)
        * score_scale
    ]
    key_grad = (
        key_grad
        + jnp.einsum("hqk,qhd->khd", score_grad, queries, preferred_element_type=jnp.float32)
        * score_scale
    )
    query_grad = jnp.concatenate(query_parts, axis=0).reshape(row_count, model_width)
    return jnp.concatenate(
        [
            query_grad,
            key_grad.reshape(row_count, model_width),
            value_grad.reshape(row_count, model_width),
        ],
        axis=1,
    )


def swap(block, axis, bit):
    return lax.ppermute(block, axis, [(i, i ^ bit) for i in range(lax.axis_size(axis))])


def turn(block, axis, step):
    size = lax.axis_size(axis)
    return lax.ppermute(block, axis, [((i + step) % size, i) for i in range(size)])


def one_way(block, axis, source, target):
    return lax.ppermute(block, axis, [(source, target)])


def place_kernel(where_ref, *refs):
    pieces, whole, sems = refs[:-2], refs[-2], refs[-1]
    section, turned, core, side = (where_ref[i] for i in range(4))
    copies = []
    for half in range(2):
        rank_core = core if half == 0 else 1 - core
        plain, over_x, over_y, far_low, far_high = pieces[half * 5 : half * 5 + 5]
        parts = [(plain, 0, section, side), (over_x, 0, 1 - section, side)]
        parts += [(over_y, 0, section, 1 - side)]
        parts += [(far_low, 0, 1 - section, 1 - side), (far_high, 2, 1 - section, 1 - side)]
        for piece, first, to_section, to_side in parts:
            for i in range(piece.shape[0]):
                shard = lax.rem(turned + first + i, 4)
                copies.append(
                    pltpu.make_async_copy(
                        piece.at[i],
                        whole.at[to_section, shard, rank_core * 2 + to_side],
                        sems.at[len(copies)],
                    )
                )
    for copy in copies:
        copy.start()
    for copy in copies:
        copy.wait()


def place(pieces, where):
    rows, columns = pieces[0].shape[1:]
    whole = jax.ShapeDtypeStruct((2, 4, 4, rows, columns), pieces[0].dtype)
    return pl.pallas_call(
        place_kernel,
        out_shape=whole,
        in_specs=[pl.BlockSpec(memory_space=pltpu.SMEM)]
        + [pl.BlockSpec(memory_space=pl.ANY)] * len(pieces),
        out_specs=pl.BlockSpec(memory_space=pl.ANY),
        scratch_shapes=[pltpu.SemaphoreType.DMA((32,))],
    )(where, *pieces)


def gather_whole(own, where):
    chunks = jnp.stack([own] + [turn(own, "shard", i) for i in (1, 2, 3)])
    over_x = swap(chunks, "section", 1)
    over_y = swap(chunks, "replica", 2)
    far_low = swap(over_x[:2], "replica", 2)
    far_high = swap(over_y[2:], "section", 1)
    mine = (chunks, over_x, over_y, far_low, far_high)
    theirs = tuple(swap(piece, "replica", 1) for piece in mine)
    return place(mine + theirs, where)


def add_low(first, second):
    return (first.astype(jnp.float32) + second.astype(jnp.float32)).astype(jnp.bfloat16)


def pick(array, index, axis):
    return lax.dynamic_index_in_dim(array, index, axis, keepdims=False)


def grad_halves(left, right, core):
    row_count, width = left.shape
    split = left.reshape(row_count, 4, 2, width // 8)
    theirs = contract_rows(pick(split, 1 - core, 2).reshape(row_count, width // 2), right)
    received = swap(theirs.astype(jnp.bfloat16), "replica", 1)
    own = contract_rows(pick(split, core, 2).reshape(row_count, width // 2), right)
    own = (own + received.astype(jnp.float32)).astype(jnp.bfloat16)
    return own.reshape(4, 2, width // 16, right.shape[1])


def halve(array, index, axis):
    size = array.shape[axis] // 2
    return lax.dynamic_slice_in_dim(array, index * size, size, axis)


def plane_reduce(mine, section, side, shard):
    low, high = mine[:2], mine[2:]
    low_got = swap(halve(low, 1 - section, 3), "section", 1)
    high_got = swap(pick(high, 1 - side, 1), "replica", 2)
    low = add_low(halve(low, section, 3), low_got)
    high = add_low(pick(high, side, 1), high_got)
    low_got = swap(pick(low, 1 - side, 1), "replica", 2)
    high_got = swap(halve(high, 1 - section, 2), "section", 1)
    low = add_low(pick(low, side, 1), low_got)
    high = add_low(halve(high, section, 2), high_got)
    both = jnp.concatenate([low, high], axis=0)
    total = pick(both, shard, 0).astype(jnp.float32)
    for i in (1, 2, 3):
        total = total + turn(pick(both, (shard - i) % 4, 0), "shard", i).astype(jnp.float32)
    return total.astype(jnp.bfloat16)


def ordered(own, other, index, axis):
    first = jnp.where(index == 0, own, other)
    second = jnp.where(index == 0, other, own)
    return jnp.concatenate([first, second], axis=axis)


def spread_back(parts, section, core, side):
    keep = jnp.where(section == 0, parts[0], parts[1])
    give = jnp.where(section == 0, parts[1], parts[0])
    rows = ordered(keep, swap(give, "section", 1), section, 1)
    rows = ordered(rows, swap(rows, "replica", 2), side, 0)
    rows = ordered(rows, swap(rows, "replica", 1), core, 0)
    return rows.astype(jnp.float32)


def total_all(array):
    for axis, bits in (("replica", 1), ("section", 1), ("replica", 2), ("shard", 1), ("shard", 2)):
        array = array + swap(array, axis, bits)
    return array


def block_forward(params_here, hidden_low, segment, living):
    (
        attention_gain,
        attention_shift,
        input_weight,
        query_bias,
        value_bias,
        output_weight,
        output_bias,
        feedforward_gain,
        feedforward_shift,
        expand_weight,
        expand_bias,
        contract_weight,
        contract_bias,
    ) = params_here
    hidden = hidden_low.astype(jnp.float32)
    normed = layer_norm(hidden, attention_gain, attention_shift).astype(jnp.bfloat16)
    joint_bias = jnp.concatenate([query_bias, jnp.zeros_like(query_bias), value_bias])
    joint_low = (
        jnp.dot(normed, input_weight, preferred_element_type=jnp.float32) + joint_bias
    ).astype(jnp.bfloat16)
    mixed, log_sums = attend_forward(joint_low, segment)
    mixed_low = mixed.astype(jnp.bfloat16)
    middle = (
        hidden + jnp.dot(mixed_low, output_weight, preferred_element_type=jnp.float32) + output_bias
    )
    normed_two = layer_norm(middle, feedforward_gain, feedforward_shift).astype(jnp.bfloat16)
    expanded = jnp.dot(normed_two, expand_weight, preferred_element_type=jnp.float32) + expand_bias
    activated = gelu_tanh(expanded).astype(jnp.bfloat16)
    result = (
        middle
        + jnp.dot(activated, contract_weight, preferred_element_type=jnp.float32)
        + contract_bias
    )
    result = result * living[:, None]
    return (
        result.astype(jnp.bfloat16),
        (hidden_low, normed, joint_low, log_sums, mixed_low, middle, normed_two, expanded, activated),
    )


def block_backward(params_here, kept_state, upstream, segment, living, grad_of):
    (
        attention_gain,
        attention_shift,
        input_weight,
        query_bias,
        value_bias,
        output_weight,
        output_bias,
        feedforward_gain,
        feedforward_shift,
        expand_weight,
        expand_bias,
        contract_weight,
        contract_bias,
    ) = params_here
    (hidden_low, normed, joint_low, log_sums, mixed_low, middle, normed_two, expanded, activated) = (
        kept_state
    )
    model_width = middle.shape[1]
    out_grad = upstream * living[:, None]
    contract_grad_low = out_grad.astype(jnp.bfloat16)
    contract_weight_grad = grad_of(activated, contract_grad_low)
    contract_bias_grad = jnp.sum(contract_grad_low.astype(jnp.float32), axis=0)
    activated_grad = times_transpose(contract_grad_low, contract_weight)
    _, gelu_pull = jax.vjp(gelu_tanh, expanded)
    (expanded_grad,) = gelu_pull(activated_grad)
    expanded_grad_low = expanded_grad.astype(jnp.bfloat16)
    expand_weight_grad = grad_of(normed_two, expanded_grad_low)
    expand_bias_grad = jnp.sum(expanded_grad_low.astype(jnp.float32), axis=0)
    normed_two_grad = times_transpose(expanded_grad_low, expand_weight)
    _, norm_two_pull = jax.vjp(layer_norm, middle, feedforward_gain, feedforward_shift)
    middle_norm_grad, feedforward_gain_grad, feedforward_shift_grad = norm_two_pull(normed_two_grad)
    middle_grad = out_grad + middle_norm_grad
    branch_grad_low = middle_grad.astype(jnp.bfloat16)
    output_weight_grad = grad_of(mixed_low, branch_grad_low)
    output_bias_grad = jnp.sum(branch_grad_low.astype(jnp.float32), axis=0)
    mixed_grad_low = times_transpose(branch_grad_low, output_weight).astype(jnp.bfloat16)
    joint_grad_low = attend_backward(joint_low, log_sums, mixed_grad_low, segment).astype(
        jnp.bfloat16
    )
    input_weight_grad = grad_of(normed, joint_grad_low)
    joint_sums = jnp.sum(joint_grad_low.astype(jnp.float32), axis=0)
    query_bias_grad = joint_sums[:model_width]
    value_bias_grad = joint_sums[2 * model_width :]
    normed_grad = times_transpose(joint_grad_low, input_weight)
    _, norm_one_pull = jax.vjp(
        layer_norm, hidden_low.astype(jnp.float32), attention_gain, attention_shift
    )
    hidden_norm_grad, attention_gain_grad, attention_shift_grad = norm_one_pull(normed_grad)
    hidden_grad = middle_grad + hidden_norm_grad
    small = jnp.concatenate(
        [
            attention_gain_grad,
            attention_shift_grad,
            query_bias_grad,
            value_bias_grad,
            output_bias_grad,
            feedforward_gain_grad,
            feedforward_shift_grad,
            contract_bias_grad,
            expand_bias_grad,
        ]
    )
    large = (input_weight_grad, output_weight_grad, expand_weight_grad, contract_weight_grad)
    return (hidden_grad, small, large)


def per_device(
    tokens,
    cotangent,
    lengths,
    assignment,
    attention_gain,
    attention_shift,
    input_weight,
    query_bias,
    value_bias,
    output_weight,
    output_bias,
    feedforward_gain,
    feedforward_shift,
    expand_weight,
    expand_bias,
    contract_weight,
    contract_bias,
):
    section = lax.axis_index("section")
    shard = lax.axis_index("shard")
    replica = lax.axis_index("replica")
    shards, replicas = lax.axis_size("shard"), lax.axis_size("replica")
    core, side = replica % 2, replica // 2
    model_width = tokens.shape[1]
    cube = shards == 4 and replicas == 4
    where = jnp.stack([section, shard, core, side]).astype(jnp.int32)

    slot = (shard * replicas + replica) * MICRO + section
    matches = (assignment == slot).astype(jnp.int32)
    counts = jnp.sum(matches[:, None] * lengths, axis=0, dtype=jnp.int32)
    segment, living = slot_layout(counts, ROWS)
    entering = lax.dynamic_slice_in_dim(tokens, section * ROWS, ROWS, 0)
    seed = lax.dynamic_slice_in_dim(cotangent, section * ROWS, ROWS, 0)

    vectors = (
        attention_gain,
        attention_shift,
        query_bias,
        value_bias,
        output_bias,
        feedforward_gain,
        feedforward_shift,
        contract_bias,
        expand_bias,
    )
    small_own = jnp.concatenate([member[0] for member in vectors])
    small_rows = small_own.shape[0] // model_width

    if cube:

        def chunk(weight):
            size = weight.shape[1] // 4
            return lax.dynamic_slice_in_dim(weight[0], (core * 2 + side) * size, size, 0)

        out_chunk = chunk(output_weight)
        out_rows = out_chunk.shape[0]
        padded = jnp.zeros((16, model_width), jnp.bfloat16)
        padded = padded.at[:small_rows].set(small_own.reshape(small_rows, model_width))
        first = gather_whole(jnp.concatenate([out_chunk, padded], axis=0), where)
        small_all = first[:, :, 0, out_rows : out_rows + small_rows].reshape(2, shards, -1)
        output_all = first[:, :, :, :out_rows].reshape(2, -1, model_width)

        def whole(weight):
            return gather_whole(chunk(weight), where).reshape(2, -1, weight.shape[2])

        input_all, expand_all, contract_all = (
            whole(input_weight),
            whole(expand_weight),
            whole(contract_weight),
        )
    else:

        def whole(weight):
            held = lax.all_gather(weight, "shard", axis=1, tiled=True)
            return lax.all_gather(held, "section", axis=0, tiled=True)

        input_all, output_all, expand_all, contract_all = (
            whole(input_weight),
            whole(output_weight),
            whole(expand_weight),
            whole(contract_weight),
        )
        small_all = whole(small_own[None, None])

    pieces = []
    start = 0
    for member in vectors:
        size = member.shape[1]
        pieces.append(small_all[:, :, start : start + size].reshape(2, -1).astype(jnp.float32))
        start += size
    (gain_a, shift_a, bias_q, bias_v, bias_o, gain_f, shift_f, bias_c, bias_e) = pieces
    params_of = [
        (
            gain_a[block],
            shift_a[block],
            input_all[block],
            bias_q[block],
            bias_v[block],
            output_all[block],
            bias_o[block],
            gain_f[block],
            shift_f[block],
            expand_all[block],
            bias_e[block],
            contract_all[block],
            bias_c[block],
        )
        for block in range(2)
    ]

    middle_out, kept_first = block_forward(params_of[0], entering, segment, living)
    last_out, kept_second = block_forward(params_of[1], middle_out, segment, living)

    if cube:

        def grad_of(left, right):
            return plane_reduce(grad_halves(left, right, core), section, side, shard)
    else:

        def grad_of(left, right):
            return contract_rows(left, right).astype(jnp.bfloat16)

    second_grad, small_second, large_second = block_backward(
        params_of[1], kept_second, seed.astype(jnp.float32), segment, living, grad_of
    )
    upstream = second_grad.astype(jnp.bfloat16).astype(jnp.float32)
    first_grad, small_first, large_first = block_backward(
        params_of[0], kept_first, upstream, segment, living, grad_of
    )

    def own_block(first_value, second_value):
        first_got = one_way(first_value, "section", 1, 0)
        second_got = one_way(second_value, "section", 0, 1)
        keep = jnp.where(section == 0, first_value, second_value)
        got = jnp.where(section == 0, first_got, second_got)
        return ordered(keep, got, section, 0)

    block_out = own_block(middle_out, last_out)
    grads_low = (first_grad.astype(jnp.bfloat16), second_grad.astype(jnp.bfloat16))
    grad_out = own_block(*grads_low).astype(jnp.float32)

    small_both = jnp.stack([small_first, small_second])
    if cube:
        small_sum = total_all(small_both.reshape(2, -1, model_width))
        small_sum = small_sum.reshape(2, -1)
        large = [
            spread_back(parts, section, core, side) for parts in zip(large_first, large_second)
        ]
    else:
        small_sum = lax.psum(small_both, ("section", "shard", "replica"))
        large = []
        for parts in zip(large_first, large_second):
            held = lax.psum_scatter(
                jnp.stack(parts), "section", scatter_dimension=0, tiled=True
            )
            held = lax.psum_scatter(held[0], "shard", scatter_dimension=0, tiled=True)
            large.append(lax.psum(held, "replica").astype(jnp.float32))
    small_sum = pick(small_sum, section, 0)
    small = []
    start = 0
    for member in vectors:
        size = member.shape[1] * shards
        part = small_sum[start : start + size].reshape(shards, -1)
        small.append(pick(part, shard, 0)[None])
        start += size
    input_grad, output_grad, expand_grad, contract_grad = (member[None] for member in large)
    return (
        block_out[None],
        grad_out[None],
        small[0],
        small[1],
        input_grad,
        small[2],
        small[3],
        output_grad,
        small[4],
        small[5],
        small[6],
        expand_grad,
        small[8],
        contract_grad,
        small[7],
    )


def solution(mesh):
    placed = (
        P(("shard", "replica"), None),
        P(("shard", "replica"), None),
        P(),
        P(),
        P("section", "shard"),
        P("section", "shard"),
        P("section", "shard", None),
        P("section", "shard"),
        P("section", "shard"),
        P("section", "shard", None),
        P("section", "shard"),
        P("section", "shard"),
        P("section", "shard"),
        P("section", "shard", None),
        P("section", "shard"),
        P("section", "shard", None),
        P("section", "shard"),
    )
    return jax.shard_map(
        per_device,
        mesh=mesh,
        in_specs=placed,
        out_specs=(
            P("section", ("shard", "replica"), None),
            P("section", ("shard", "replica"), None),
            P("section", "shard"),
            P("section", "shard"),
            P("section", "shard", None),
            P("section", "shard"),
            P("section", "shard"),
            P("section", "shard", None),
            P("section", "shard"),
            P("section", "shard"),
            P("section", "shard"),
            P("section", "shard", None),
            P("section", "shard"),
            P("section", "shard", None),
            P("section", "shard"),
        ),
        check_vma=False,
    )
```

```python
import functools

import jax
import jax.numpy as jnp
from jax import lax
from jax.experimental import pallas as pl
from jax.experimental.pallas import tpu as pltpu
from jax.sharding import PartitionSpec as P

HEADS = 12
ROWS = 512
MICRO = 2


EPSILON = 1e-05
MASKED_SCORE = -1e30


def layer_norm(hidden, norm_gain, norm_shift):
    center = hidden - jnp.mean(hidden, axis=-1, keepdims=True)
    spread = jnp.mean(center * center, axis=-1, keepdims=True)
    return center * lax.rsqrt(spread + EPSILON) * norm_gain + norm_shift


def slot_layout(counts, row_count):
    bounds = jnp.cumsum(counts, dtype=jnp.int32)
    places = jnp.arange(row_count, dtype=jnp.int32)
    segment = jnp.sum(
        (bounds[None, :] <= places[:, None]).astype(jnp.int32), axis=1, dtype=jnp.int32
    )
    living = (places < bounds[-1]).astype(jnp.float32)
    return (segment, living)


def gelu_tanh(values):
    return jax.nn.gelu(values, approximate=True)


def contract_rows(left_side, right_side):
    return lax.dot_general(
        left_side, right_side, (((0,), (0,)), ((), ())), preferred_element_type=jnp.float32
    )


def times_transpose(left_side, right_side):
    return lax.dot_general(
        left_side, right_side, (((1,), (1,)), ((), ())), preferred_element_type=jnp.float32
    )


def masked_bias(segment_column, segment_row):
    row_count = segment_column.shape[0]
    query_places = lax.broadcasted_iota(jnp.int32, (row_count, row_count), 0)
    key_places = lax.broadcasted_iota(jnp.int32, (row_count, row_count), 1)
    allowed = (segment_column == segment_row) & (key_places <= query_places)
    return jnp.where(allowed, 0.0, MASKED_SCORE)


def head_lanes(block, head):
    half = block.shape[1] // 2
    lanes = lax.broadcasted_iota(jnp.int32, block.shape, 1)
    return jnp.where((lanes < half) == (head == 0), block, jnp.zeros_like(block))


def attend_kernel(column_ref, row_ref, q_ref, k_ref, v_ref, mixed_ref, log_ref, bias_ref):
    @pl.when(pl.program_id(0) == 0)
    def _():
        bias_ref[...] = masked_bias(column_ref[...], row_ref[...])

    row_count, width = q_ref.shape
    tall = row_count // 2
    scale = (width // 2) ** (-0.5)
    first_lanes = lax.broadcasted_iota(jnp.int32, (tall, width), 1) < width // 2
    for start in (0, tall):
        stop = start + tall
        queries = q_ref[start:stop] * jnp.asarray(scale, q_ref.dtype)
        outs, logs = [], []
        for head in range(2):
            scores = times_transpose(head_lanes(queries, head), k_ref[:stop])
            scores = scores + bias_ref[start:stop, :stop]
            row_max = jnp.max(scores, axis=1, keepdims=True)
            exponent = jnp.exp(scores - row_max)
            row_total = jnp.sum(exponent, axis=1, keepdims=True)
            probs = (exponent * (1.0 / row_total)).astype(jnp.bfloat16)
            outs.append(jnp.dot(probs, v_ref[:stop], preferred_element_type=jnp.float32))
            logs.append(jnp.broadcast_to(row_max + jnp.log(row_total), (tall, width)))
        mixed_ref[start:stop] = jnp.where(first_lanes, *outs).astype(jnp.bfloat16)
        log_ref[start:stop] = jnp.where(first_lanes, *logs)


def attend_back_kernel(
    column_ref, row_ref, q_ref, k_ref, v_ref, grad_ref, log_ref, dq_ref, dk_ref, dv_ref, bias_ref
):
    @pl.when(pl.program_id(0) == 0)
    def _():
        bias_ref[...] = masked_bias(column_ref[...], row_ref[...])

    row_count, width = q_ref.shape
    tall = row_count // 2
    scale = (width // 2) ** (-0.5)
    first_lanes = lax.broadcasted_iota(jnp.int32, (tall, width), 1) < width // 2
    key_parts, value_parts = [], []
    for start in (0, tall):
        stop = start + tall
        queries = q_ref[start:stop] * jnp.asarray(scale, q_ref.dtype)
        query_parts = []
        key_grad = value_grad = 0.0
        for head in range(2):
            mine = head_lanes(queries, head)
            grad = head_lanes(grad_ref[start:stop], head)
            lane = head * (width // 2)
            scores = times_transpose(mine, k_ref[:stop]) + bias_ref[start:stop, :stop]
            probs = jnp.exp(scores - log_ref[start:stop, lane : lane + 1])
            prob_grad = times_transpose(grad, v_ref[:stop])
            center = jnp.sum(prob_grad * probs, axis=1, keepdims=True)
            score_grad = (probs * (prob_grad - center)).astype(jnp.bfloat16)
            query_parts.append(
                jnp.dot(score_grad, k_ref[:stop], preferred_element_type=jnp.float32)
            )
            key_grad = key_grad + contract_rows(score_grad, mine)
            value_grad = value_grad + contract_rows(probs.astype(jnp.bfloat16), grad)
        dq_ref[start:stop] = (jnp.where(first_lanes, *query_parts) * scale).astype(jnp.bfloat16)
        key_parts.append(key_grad)
        value_parts.append(value_grad)
    for parts, target in ((key_parts, dk_ref), (value_parts, dv_ref)):
        target[:tall] = (parts[0] + parts[1][:tall]).astype(jnp.bfloat16)
        target[tall:] = parts[1][tall:].astype(jnp.bfloat16)


def attention_call(kernel, segment, blocks, outs, flops):
    row_count = segment.shape[0]
    pairs = HEADS // 2
    model_width = blocks[0][0].shape[1] // 3
    lanes = model_width // pairs

    def spec(first):
        return pl.BlockSpec((row_count, lanes), lambda pair: (0, first + pair))

    return pl.pallas_call(
        kernel,
        grid=(pairs,),
        out_shape=[jax.ShapeDtypeStruct((row_count, model_width), kind) for kind in outs],
        in_specs=[
            pl.BlockSpec((row_count, 1), lambda pair: (0, 0)),
            pl.BlockSpec((1, row_count), lambda pair: (0, 0)),
        ]
        + [spec(first) for _, first in blocks],
        out_specs=[spec(0) for _ in outs],
        scratch_shapes=[pltpu.VMEM((row_count, row_count), jnp.float32)],
        compiler_params=pltpu.CompilerParams(vmem_limit_bytes=48 * 1024 * 1024),
        cost_estimate=pl.CostEstimate(
            flops=flops * row_count * row_count * model_width,
            bytes_accessed=row_count * model_width * 16,
            transcendentals=HEADS * row_count * row_count,
        ),
    )(segment[:, None], segment[None, :], *(array for array, _ in blocks))


def attend_forward(joint_low, segment):
    pairs = HEADS // 2
    blocks = [(joint_low, first * pairs) for first in range(3)]
    return attention_call(attend_kernel, segment, blocks, (jnp.bfloat16, jnp.float32), 8)


def attend_backward(joint_low, log_sums, mixed_grad, segment):
    pairs = HEADS // 2
    blocks = [(joint_low, first * pairs) for first in range(3)]
    blocks += [(mixed_grad, 0), (log_sums, 0)]
    parts = attention_call(attend_back_kernel, segment, blocks, (jnp.bfloat16,) * 3, 20)
    return jnp.concatenate(parts, axis=1)


def swap(block, axis, bit):
    return lax.ppermute(block, axis, [(i, i ^ bit) for i in range(lax.axis_size(axis))])


def turn(block, axis, step):
    size = lax.axis_size(axis)
    return lax.ppermute(block, axis, [((i + step) % size, i) for i in range(size)])


def one_way(block, axis, source, target):
    return lax.ppermute(block, axis, [(source, target)])


def place_kernel(rows, extra, where_ref, *refs):
    pieces, outs, held, in_sems, out_sems = refs[:10], refs[10:-3], refs[-3], refs[-2], refs[-1]
    section, turned, core, side = (where_ref[i] for i in range(4))

    def run(same, other):
        steps = []
        for half in range(2):
            rank_core = core if half == 0 else 1 - core
            plain, over_x, over_y, far_low, far_high = pieces[half * 5 : half * 5 + 5]
            parts = [(plain, 0, same, side), (over_x, 0, other, side), (over_y, 0, same, 1 - side)]
            parts += [(far_low, 0, other, 1 - side), (far_high, 2, other, 1 - side)]
            for place_index, (piece, first, block, to_side) in enumerate(parts):
                for i in range(piece.shape[0]):
                    shard = lax.rem(turned + first + i, 4)
                    slot = held.at[len(steps)]
                    load = pltpu.make_async_copy(piece.at[i], slot, in_sems.at[len(steps)])
                    load.start()
                    target = outs[block].at[shard, rank_core * 2 + to_side]
                    stores = [(slot.at[:rows], target)]
                    if extra and half == 0 and place_index < 2:
                        stores.append((slot.at[rows:], outs[2 + block].at[shard]))
                    steps.append((load, stores))
        begun = []
        for load, stores in steps:
            load.wait()
            for source, target in stores:
                store = pltpu.make_async_copy(source, target, out_sems.at[len(begun)])
                store.start()
                begun.append(store)
        for store in begun:
            store.wait()

    @pl.when(section == 0)
    def _():
        run(0, 1)

    @pl.when(section == 1)
    def _():
        run(1, 0)


def place(pieces, where, extra=0):
    rows, columns = pieces[0].shape[1:]
    kind = pieces[0].dtype
    keep = rows - extra
    shapes = [jax.ShapeDtypeStruct((4, 4, keep, columns), kind)] * 2
    if extra:
        shapes += [jax.ShapeDtypeStruct((4, extra, columns), kind)] * 2
    return pl.pallas_call(
        functools.partial(place_kernel, keep, extra),
        out_shape=shapes,
        in_specs=[pl.BlockSpec(memory_space=pltpu.SMEM)]
        + [pl.BlockSpec(memory_space=pl.ANY)] * len(pieces),
        out_specs=[pl.BlockSpec(memory_space=pl.ANY)] * len(shapes),
        scratch_shapes=[
            pltpu.VMEM((32, rows, columns), kind),
            pltpu.SemaphoreType.DMA((32,)),
            pltpu.SemaphoreType.DMA((40,)),
        ],
        compiler_params=pltpu.CompilerParams(vmem_limit_bytes=32 * 1024 * 1024),
    )(where, *pieces)


def gather_along(own):
    return jnp.stack([own] + [turn(own, "shard", i) for i in (1, 2, 3)])


def gather_across(chunks):
    return (chunks, swap(chunks, "section", 1), swap(chunks, "replica", 2))


def gather_far(chunks, over_x, over_y):
    far_low = swap(over_x[:2], "replica", 2)
    far_high = swap(over_y[2:], "section", 1)
    return (chunks, over_x, over_y, far_low, far_high)


def gather_mate(*mine):
    return mine + tuple(swap(piece, "replica", 1) for piece in mine)


def gather_all(chunks):
    steps = (gather_along, gather_across, gather_far, gather_mate)
    states = [(chunk,) for chunk in chunks]
    for turn_index in range(len(chunks) + len(steps) - 1):
        states = lax.optimization_barrier(states)
        for index in range(len(chunks)):
            step = turn_index - index
            if 0 <= step < len(steps):
                result = steps[step](*states[index])
                states[index] = result if isinstance(result, tuple) else (result,)
    return states


def add_low(first, second):
    return (first.astype(jnp.float32) + second.astype(jnp.float32)).astype(jnp.bfloat16)


def pick(array, index, axis):
    return lax.dynamic_index_in_dim(array, index, axis, keepdims=False)


def grad_share(left, right, core):
    whole = contract_rows(left, right).astype(jnp.bfloat16)
    rows, columns = whole.shape
    halves = whole.reshape(4, 2, rows // 8, columns)
    received = swap(pick(halves, 1 - core, 1), "replica", 1)
    return add_low(pick(halves, core, 1), received).reshape(4, 2, rows // 16, columns)


def halve(array, index, axis):
    size = array.shape[axis] // 2
    return lax.dynamic_slice_in_dim(array, index * size, size, axis)


def reduce_steps(section, side, shard):
    def across(mine):
        low, high = mine[:2], mine[2:]
        low_got = swap(halve(low, 1 - section, 3), "section", 1)
        high_got = swap(pick(high, 1 - side, 1), "replica", 2)
        return (halve(low, section, 3), pick(high, side, 1), low_got, high_got)

    def along(low, high, low_got, high_got):
        low, high = add_low(low, low_got), add_low(high, high_got)
        low_got = swap(pick(low, 1 - side, 1), "replica", 2)
        high_got = swap(halve(high, 1 - section, 2), "section", 1)
        return (pick(low, side, 1), halve(high, section, 2), low_got, high_got)

    def over_shards(low, high, low_got, high_got):
        both = jnp.concatenate([add_low(low, low_got), add_low(high, high_got)], axis=0)
        got = [turn(pick(both, (shard - i) % 4, 0), "shard", i) for i in (1, 2, 3)]
        return (pick(both, shard, 0), *got)

    def finish(own, *got):
        total = own.astype(jnp.float32)
        for member in got:
            total = total + member.astype(jnp.float32)
        return (total.astype(jnp.bfloat16),)

    return (across, along, over_shards, finish)


def spread_steps(section, core, side):
    def back(first, second):
        keep = jnp.where(section == 0, first, second)
        give = jnp.where(section == 0, second, first)
        return (keep, swap(give, "section", 1))

    def sides(keep, got):
        rows = ordered(keep, got, section, 1)
        return (rows, swap(rows, "replica", 2))

    def cores(own, got):
        rows = ordered(own, got, side, 0)
        return (rows, swap(rows, "replica", 1))

    def finish(own, got):
        return (ordered(own, got, core, 0).astype(jnp.float32),)

    return (back, sides, cores, finish)


class Flows:
    def __init__(self, reduce_steps, spread_steps):
        self.reduce_steps = reduce_steps
        self.spread_steps = spread_steps
        self.left = {}
        self.states = {}

    def add(self, name, mine):
        self.left[name] = list(self.reduce_steps)
        self.states[name] = (mine,)

    def join(self):
        for name in [name for name in self.left if name.startswith("first_")]:
            whole, other = name[len("first_") :], "second_" + name[len("first_") :]
            if not self.left[name] and not self.left[other] and whole not in self.left:
                self.left[whole] = list(self.spread_steps)
                self.states[whole] = self.states[name] + self.states[other]

    def busy(self):
        return [name for name in self.left if self.left[name]]

    def stage(self, compute, *inputs):
        self.join()
        names = self.busy()
        states = [self.states[name] for name in names]
        inputs, states = lax.optimization_barrier((inputs, states))
        moved = [self.left[name].pop(0)(*state) for name, state in zip(names, states)]
        results, moved = lax.optimization_barrier((compute(*inputs), moved))
        self.states.update(zip(names, moved))
        self.join()
        return results


def ordered(own, other, index, axis):
    first = jnp.where(index == 0, own, other)
    second = jnp.where(index == 0, other, own)
    return jnp.concatenate([first, second], axis=axis)


def total_all(array):
    for axis, bits in (("replica", 1), ("section", 1), ("replica", 2), ("shard", 1), ("shard", 2)):
        array = array + swap(array, axis, bits)
    return array


def block_forward(params_here, hidden_low, segment, living):
    (
        attention_gain,
        attention_shift,
        input_weight,
        query_bias,
        value_bias,
        output_weight,
        output_bias,
        feedforward_gain,
        feedforward_shift,
        expand_weight,
        expand_bias,
        contract_weight,
        contract_bias,
    ) = params_here
    hidden = hidden_low.astype(jnp.float32)
    normed = layer_norm(hidden, attention_gain, attention_shift).astype(jnp.bfloat16)
    joint_bias = jnp.concatenate([query_bias, jnp.zeros_like(query_bias), value_bias])
    joint_low = (
        jnp.dot(normed, input_weight, preferred_element_type=jnp.float32) + joint_bias
    ).astype(jnp.bfloat16)
    mixed_low, log_sums = attend_forward(joint_low, segment)
    middle = (
        hidden + jnp.dot(mixed_low, output_weight, preferred_element_type=jnp.float32) + output_bias
    )
    normed_two = layer_norm(middle, feedforward_gain, feedforward_shift).astype(jnp.bfloat16)
    expanded = jnp.dot(normed_two, expand_weight, preferred_element_type=jnp.float32) + expand_bias
    activated = gelu_tanh(expanded).astype(jnp.bfloat16)
    result = (
        middle
        + jnp.dot(activated, contract_weight, preferred_element_type=jnp.float32)
        + contract_bias
    )
    result = result * living[:, None]
    return (
        result.astype(jnp.bfloat16),
        (hidden_low, normed, joint_low, log_sums, mixed_low, middle, normed_two, expanded, activated),
    )


def block_backward(params_here, kept_state, upstream, segment, living, flow, tag, core):
    (
        attention_gain,
        attention_shift,
        input_weight,
        query_bias,
        value_bias,
        output_weight,
        output_bias,
        feedforward_gain,
        feedforward_shift,
        expand_weight,
        expand_bias,
        contract_weight,
        contract_bias,
    ) = params_here
    (hidden_low, normed, joint_low, log_sums, mixed_low, middle, normed_two, expanded, activated) = (
        kept_state
    )
    model_width = middle.shape[1]

    def contract_part(upstream, activated):
        out_grad = upstream * living[:, None]
        low = out_grad.astype(jnp.bfloat16)
        return (out_grad, low, grad_share(activated, low, core))

    out_grad, contract_grad_low, contract_mine = flow.stage(contract_part, upstream, activated)
    flow.add(tag + "contract", contract_mine)

    def expand_part(contract_grad_low, expanded):
        activated_grad = times_transpose(contract_grad_low, contract_weight)
        _, gelu_pull = jax.vjp(gelu_tanh, expanded)
        (expanded_grad,) = gelu_pull(activated_grad)
        return expanded_grad.astype(jnp.bfloat16)

    expanded_grad_low = flow.stage(expand_part, contract_grad_low, expanded)

    def expand_grad_part(expanded_grad_low, normed_two):
        return grad_share(normed_two, expanded_grad_low, core)

    expand_mine = flow.stage(expand_grad_part, expanded_grad_low, normed_two)

    def norm_part(expanded_grad_low, out_grad, middle, mixed_low):
        normed_two_grad = times_transpose(expanded_grad_low, expand_weight)
        _, pull = jax.vjp(layer_norm, middle, feedforward_gain, feedforward_shift)
        middle_norm_grad, gain_grad, shift_grad = pull(normed_two_grad)
        middle_grad = out_grad + middle_norm_grad
        branch_grad_low = middle_grad.astype(jnp.bfloat16)
        mixed_grad_low = times_transpose(branch_grad_low, output_weight).astype(jnp.bfloat16)
        own = grad_share(mixed_low, branch_grad_low, core)
        return (middle_grad, branch_grad_low, mixed_grad_low, gain_grad, shift_grad, own)

    (
        middle_grad,
        branch_grad_low,
        mixed_grad_low,
        feedforward_gain_grad,
        feedforward_shift_grad,
        output_mine,
    ) = flow.stage(norm_part, expanded_grad_low, out_grad, middle, mixed_low)
    flow.add(tag + "expand", jnp.concatenate([expand_mine, output_mine], axis=3))

    def attention_part(joint_low, log_sums, mixed_grad_low):
        return attend_backward(joint_low, log_sums, mixed_grad_low, segment)

    joint_grad_low = flow.stage(attention_part, joint_low, log_sums, mixed_grad_low)

    def input_part(normed, joint_grad_low):
        return grad_share(normed, joint_grad_low, core)

    input_mine = flow.stage(input_part, normed, joint_grad_low)
    flow.add(tag + "input", input_mine)

    def last_part(joint_grad_low, middle_grad, hidden_low):
        normed_grad = times_transpose(joint_grad_low, input_weight)
        _, pull = jax.vjp(
            layer_norm, hidden_low.astype(jnp.float32), attention_gain, attention_shift
        )
        hidden_norm_grad, gain_grad, shift_grad = pull(normed_grad)
        return (middle_grad + hidden_norm_grad, gain_grad, shift_grad)

    hidden_grad, attention_gain_grad, attention_shift_grad = flow.stage(
        last_part, joint_grad_low, middle_grad, hidden_low
    )

    joint_sums = jnp.sum(joint_grad_low.astype(jnp.float32), axis=0)
    small = jnp.concatenate(
        [
            attention_gain_grad,
            attention_shift_grad,
            joint_sums[:model_width],
            joint_sums[2 * model_width :],
            jnp.sum(branch_grad_low.astype(jnp.float32), axis=0),
            feedforward_gain_grad,
            feedforward_shift_grad,
            jnp.sum(contract_grad_low.astype(jnp.float32), axis=0),
            jnp.sum(expanded_grad_low.astype(jnp.float32), axis=0),
        ]
    )
    return (hidden_grad, small)


def core_whole(mine, core):
    shards, sides, rows, columns = mine.shape
    own = mine.reshape(shards, 1, sides * rows, columns)
    both = jnp.concatenate([jnp.where(core == 0, own, 0), jnp.where(core == 0, 0, own)], axis=1)
    return both.reshape(shards * 2 * sides * rows, columns)


def per_device(
    tokens,
    cotangent,
    lengths,
    assignment,
    attention_gain,
    attention_shift,
    input_weight,
    query_bias,
    value_bias,
    output_weight,
    output_bias,
    feedforward_gain,
    feedforward_shift,
    expand_weight,
    expand_bias,
    contract_weight,
    contract_bias,
):
    section = lax.axis_index("section")
    shard = lax.axis_index("shard")
    replica = lax.axis_index("replica")
    shards, replicas = lax.axis_size("shard"), lax.axis_size("replica")
    core, side = replica % 2, replica // 2
    model_width = tokens.shape[1]
    cube = shards == 4 and replicas == 4
    where = jnp.stack([section, shard, core, side]).astype(jnp.int32)

    slot = (shard * replicas + replica) * MICRO + section
    matches = (assignment == slot).astype(jnp.int32)
    counts = jnp.sum(matches[:, None] * lengths, axis=0, dtype=jnp.int32)
    segment, living = slot_layout(counts, ROWS)
    entering = lax.dynamic_slice_in_dim(tokens, section * ROWS, ROWS, 0)
    seed = lax.dynamic_slice_in_dim(cotangent, section * ROWS, ROWS, 0)

    vectors = (
        attention_gain,
        attention_shift,
        query_bias,
        value_bias,
        output_bias,
        feedforward_gain,
        feedforward_shift,
        contract_bias,
        expand_bias,
    )
    small_own = jnp.concatenate([member[0] for member in vectors])
    small_rows = small_own.shape[0] // model_width

    if cube:

        def chunk(weight):
            size = weight.shape[1] // 4
            return lax.dynamic_slice_in_dim(weight[0], (core * 2 + side) * size, size, 0)

        out_chunk = chunk(output_weight)
        padded = jnp.zeros((16, model_width), jnp.bfloat16)
        padded = padded.at[:small_rows].set(small_own.reshape(small_rows, model_width))
        packed = jnp.concatenate([out_chunk, padded], axis=0)
        out_pieces, in_pieces, expand_pieces, contract_pieces = gather_all(
            [packed, chunk(input_weight), chunk(expand_weight), chunk(contract_weight)]
        )

        def joined(members):
            return [member.reshape(-1, member.shape[-1]) for member in members]

        *output_all, small_first, small_second = place(out_pieces, where, 16)
        small_all = jnp.stack([small_first, small_second])[:, :, :small_rows]
        small_all = small_all.reshape(2, shards, -1)
        output_all = joined(output_all)
        input_all = joined(place(in_pieces, where))
        expand_all = joined(place(expand_pieces, where))
        contract_all = joined(place(contract_pieces, where))
    else:

        def whole(weight):
            held = lax.all_gather(weight, "shard", axis=1, tiled=True)
            return lax.all_gather(held, "section", axis=0, tiled=True)

        input_all, output_all, expand_all, contract_all = (
            whole(input_weight),
            whole(output_weight),
            whole(expand_weight),
            whole(contract_weight),
        )
        small_all = whole(small_own[None, None])

    pieces = []
    start = 0
    for member in vectors:
        size = member.shape[1]
        pieces.append(small_all[:, :, start : start + size].reshape(2, -1).astype(jnp.float32))
        start += size
    (gain_a, shift_a, bias_q, bias_v, bias_o, gain_f, shift_f, bias_c, bias_e) = pieces
    params_of = [
        (
            gain_a[block],
            shift_a[block],
            input_all[block],
            bias_q[block],
            bias_v[block],
            output_all[block],
            bias_o[block],
            gain_f[block],
            shift_f[block],
            expand_all[block],
            bias_e[block],
            contract_all[block],
            bias_c[block],
        )
        for block in range(2)
    ]

    middle_out, kept_first = block_forward(params_of[0], entering, segment, living)
    last_out, kept_second = block_forward(params_of[1], middle_out, segment, living)

    flow = Flows(
        reduce_steps(section, side, shard) if cube else (),
        spread_steps(section, core, side) if cube else (),
    )
    second_grad, small_second = block_backward(
        params_of[1], kept_second, seed.astype(jnp.float32), segment, living, flow, "second_", core
    )
    upstream = second_grad.astype(jnp.bfloat16).astype(jnp.float32)
    first_grad, small_first = block_backward(
        params_of[0], kept_first, upstream, segment, living, flow, "first_", core
    )
    while flow.busy():
        flow.stage(lambda: ())

    def own_block(first_value, second_value):
        first_got = one_way(first_value, "section", 1, 0)
        second_got = one_way(second_value, "section", 0, 1)
        keep = jnp.where(section == 0, first_value, second_value)
        got = jnp.where(section == 0, first_got, second_got)
        return ordered(keep, got, section, 0)

    block_out = own_block(middle_out, last_out)
    grads_low = (first_grad.astype(jnp.bfloat16), second_grad.astype(jnp.bfloat16))
    grad_out = own_block(*grads_low).astype(jnp.float32)

    small_both = jnp.stack([small_first, small_second])
    if cube:
        small_sum = total_all(small_both.reshape(2, -1, model_width))
        small_sum = small_sum.reshape(2, -1)
        large = [flow.states[name][0] for name in ("input", "expand", "contract")]
    else:
        small_sum = lax.psum(small_both, ("section", "shard", "replica"))
        large = []
        for name in ("input", "expand", "contract"):
            wide = jnp.stack([core_whole(member, core) for member in flow.states[name]])
            held = lax.psum_scatter(wide, "section", scatter_dimension=0, tiled=True)
            held = lax.psum_scatter(held[0], "shard", scatter_dimension=0, tiled=True)
            large.append(lax.psum(held, "replica").astype(jnp.float32))
    small_sum = pick(small_sum, section, 0)
    small = []
    start = 0
    for member in vectors:
        size = member.shape[1] * shards
        part = small_sum[start : start + size].reshape(shards, -1)
        small.append(pick(part, shard, 0)[None])
        start += size
    input_grad, expand_both, contract_grad = (member[None] for member in large)
    expand_width = expand_weight.shape[2]
    expand_grad, output_grad = expand_both[:, :, :expand_width], expand_both[:, :, expand_width:]
    return (
        block_out[None],
        grad_out[None],
        small[0],
        small[1],
        input_grad,
        small[2],
        small[3],
        output_grad,
        small[4],
        small[5],
        small[6],
        expand_grad,
        small[8],
        contract_grad,
        small[7],
    )


def solution(mesh):
    placed = (
        P(("shard", "replica"), None),
        P(("shard", "replica"), None),
        P(),
        P(),
        P("section", "shard"),
        P("section", "shard"),
        P("section", "shard", None),
        P("section", "shard"),
        P("section", "shard"),
        P("section", "shard", None),
        P("section", "shard"),
        P("section", "shard"),
        P("section", "shard"),
        P("section", "shard", None),
        P("section", "shard"),
        P("section", "shard", None),
        P("section", "shard"),
    )
    return jax.shard_map(
        per_device,
        mesh=mesh,
        in_specs=placed,
        out_specs=(
            P("section", ("shard", "replica"), None),
            P("section", ("shard", "replica"), None),
            P("section", "shard"),
            P("section", "shard"),
            P("section", "shard", None),
            P("section", "shard"),
            P("section", "shard"),
            P("section", "shard", None),
            P("section", "shard"),
            P("section", "shard"),
            P("section", "shard"),
            P("section", "shard", None),
            P("section", "shard"),
            P("section", "shard", None),
            P("section", "shard"),
        ),
        check_vma=False,
    )
```

```python
import functools

import jax
import jax.numpy as jnp
from jax import lax
from jax.experimental import pallas as pl
from jax.experimental.pallas import tpu as pltpu
from jax.sharding import PartitionSpec as P

HEADS = 12
ROWS = 512
MICRO = 2


EPSILON = 1e-05
MASKED_SCORE = -1e30

SHORT = pl.CostEstimate(flops=1, bytes_accessed=1, transcendentals=0)


def layer_norm(hidden, norm_gain, norm_shift):
    center = hidden - jnp.mean(hidden, axis=-1, keepdims=True)
    spread = jnp.mean(center * center, axis=-1, keepdims=True)
    return center * lax.rsqrt(spread + EPSILON) * norm_gain + norm_shift


def slot_layout(counts, row_count):
    bounds = jnp.cumsum(counts, dtype=jnp.int32)
    places = jnp.arange(row_count, dtype=jnp.int32)
    segment = jnp.sum(
        (bounds[None, :] <= places[:, None]).astype(jnp.int32), axis=1, dtype=jnp.int32
    )
    living = (places < bounds[-1]).astype(jnp.float32)
    return (segment, living)


def gelu_tanh(values):
    return jax.nn.gelu(values, approximate=True)


def contract_rows(left_side, right_side):
    return lax.dot_general(
        left_side, right_side, (((0,), (0,)), ((), ())), preferred_element_type=jnp.float32
    )


def times_transpose(left_side, right_side):
    return lax.dot_general(
        left_side, right_side, (((1,), (1,)), ((), ())), preferred_element_type=jnp.float32
    )


def masked_bias(segment_column, segment_row):
    row_count = segment_column.shape[0]
    query_places = lax.broadcasted_iota(jnp.int32, (row_count, row_count), 0)
    key_places = lax.broadcasted_iota(jnp.int32, (row_count, row_count), 1)
    allowed = (segment_column == segment_row) & (key_places <= query_places)
    return jnp.where(allowed, 0.0, MASKED_SCORE)


def head_lanes(block, head):
    half = block.shape[1] // 2
    lanes = lax.broadcasted_iota(jnp.int32, block.shape, 1)
    return jnp.where((lanes < half) == (head == 0), block, jnp.zeros_like(block))


def attend_kernel(column_ref, row_ref, q_ref, k_ref, v_ref, mixed_ref, log_ref, bias_ref):
    @pl.when(pl.program_id(0) == 0)
    def _():
        bias_ref[...] = masked_bias(column_ref[...], row_ref[...])

    row_count, width = q_ref.shape
    tall = row_count // 2
    scale = (width // 2) ** (-0.5)
    first_lanes = lax.broadcasted_iota(jnp.int32, (tall, width), 1) < width // 2
    for start in (0, tall):
        stop = start + tall
        queries = q_ref[start:stop] * jnp.asarray(scale, q_ref.dtype)
        outs, logs = [], []
        for head in range(2):
            scores = times_transpose(head_lanes(queries, head), k_ref[:stop])
            scores = scores + bias_ref[start:stop, :stop]
            row_max = jnp.max(scores, axis=1, keepdims=True)
            exponent = jnp.exp(scores - row_max)
            row_total = jnp.sum(exponent, axis=1, keepdims=True)
            probs = (exponent * (1.0 / row_total)).astype(jnp.bfloat16)
            outs.append(jnp.dot(probs, v_ref[:stop], preferred_element_type=jnp.float32))
            logs.append(jnp.broadcast_to(row_max + jnp.log(row_total), (tall, width)))
        mixed_ref[start:stop] = jnp.where(first_lanes, *outs).astype(jnp.bfloat16)
        log_ref[start:stop] = jnp.where(first_lanes, *logs)


def attend_back_kernel(
    column_ref, row_ref, q_ref, k_ref, v_ref, grad_ref, log_ref, dq_ref, dk_ref, dv_ref, bias_ref
):
    @pl.when(pl.program_id(0) == 0)
    def _():
        bias_ref[...] = masked_bias(column_ref[...], row_ref[...])

    row_count, width = q_ref.shape
    tall = row_count // 2
    scale = (width // 2) ** (-0.5)
    first_lanes = lax.broadcasted_iota(jnp.int32, (tall, width), 1) < width // 2
    key_parts, value_parts = [], []
    for start in (0, tall):
        stop = start + tall
        queries = q_ref[start:stop] * jnp.asarray(scale, q_ref.dtype)
        query_parts = []
        key_grad = value_grad = 0.0
        for head in range(2):
            mine = head_lanes(queries, head)
            grad = head_lanes(grad_ref[start:stop], head)
            lane = head * (width // 2)
            scores = times_transpose(mine, k_ref[:stop]) + bias_ref[start:stop, :stop]
            probs = jnp.exp(scores - log_ref[start:stop, lane : lane + 1])
            prob_grad = times_transpose(grad, v_ref[:stop])
            center = jnp.sum(prob_grad * probs, axis=1, keepdims=True)
            score_grad = (probs * (prob_grad - center)).astype(jnp.bfloat16)
            query_parts.append(
                jnp.dot(score_grad, k_ref[:stop], preferred_element_type=jnp.float32)
            )
            key_grad = key_grad + contract_rows(score_grad, mine)
            value_grad = value_grad + contract_rows(probs.astype(jnp.bfloat16), grad)
        dq_ref[start:stop] = (jnp.where(first_lanes, *query_parts) * scale).astype(jnp.bfloat16)
        key_parts.append(key_grad)
        value_parts.append(value_grad)
    for parts, target in ((key_parts, dk_ref), (value_parts, dv_ref)):
        target[:tall] = (parts[0] + parts[1][:tall]).astype(jnp.bfloat16)
        target[tall:] = parts[1][tall:].astype(jnp.bfloat16)


def attention_call(kernel, segment, blocks, outs):
    row_count = segment.shape[0]
    pairs = HEADS // 2
    model_width = blocks[0][0].shape[1] // 3
    lanes = model_width // pairs

    def spec(first):
        return pl.BlockSpec((row_count, lanes), lambda pair: (0, first + pair))

    return pl.pallas_call(
        kernel,
        grid=(pairs,),
        out_shape=[jax.ShapeDtypeStruct((row_count, model_width), kind) for kind in outs],
        in_specs=[
            pl.BlockSpec((row_count, 1), lambda pair: (0, 0)),
            pl.BlockSpec((1, row_count), lambda pair: (0, 0)),
        ]
        + [spec(first) for _, first in blocks],
        out_specs=[spec(0) for _ in outs],
        scratch_shapes=[pltpu.VMEM((row_count, row_count), jnp.float32)],
        compiler_params=pltpu.CompilerParams(vmem_limit_bytes=48 * 1024 * 1024),
        cost_estimate=SHORT,
    )(segment[:, None], segment[None, :], *(array for array, _ in blocks))


def attend_forward(joint_low, segment):
    pairs = HEADS // 2
    blocks = [(joint_low, first * pairs) for first in range(3)]
    return attention_call(attend_kernel, segment, blocks, (jnp.bfloat16, jnp.float32))


def attend_backward(joint_low, log_sums, mixed_grad, segment):
    pairs = HEADS // 2
    blocks = [(joint_low, first * pairs) for first in range(3)]
    blocks += [(mixed_grad, 0), (log_sums, 0)]
    parts = attention_call(attend_back_kernel, segment, blocks, (jnp.bfloat16,) * 3)
    return jnp.concatenate(parts, axis=1)


def swap(block, axis, bit):
    return lax.ppermute(block, axis, [(i, i ^ bit) for i in range(lax.axis_size(axis))])


def turn(block, axis, step):
    size = lax.axis_size(axis)
    return lax.ppermute(block, axis, [((i + step) % size, i) for i in range(size)])


def one_way(block, axis, source, target):
    return lax.ppermute(block, axis, [(source, target)])


def place_kernel(widths, where_ref, mine, theirs, *refs):
    outs, held, in_sems, out_sems = refs[:-3], refs[-3], refs[-2], refs[-1]
    section, core, side = (where_ref[i] for i in range(3))

    def run(same, other):
        steps = []
        for rank_core, pieces in ((core, mine), (1 - core, theirs)):
            for i in range(16):
                block = (same, other, same, other)[i // 4]
                to_side = (side, side, 1 - side, 1 - side)[i // 4]
                slot = held.at[len(steps)]
                load = pltpu.make_async_copy(pieces.at[i], slot, in_sems.at[len(steps)])
                load.start()
                stores, start = [], 0
                for index, width in enumerate(widths):
                    target = outs[block * len(widths) + index].at[i % 4, rank_core * 2 + to_side]
                    stores.append((slot.at[:, start : start + width], target))
                    start += width
                steps.append((load, stores))
        begun = []
        for load, stores in steps:
            load.wait()
            for source, target in stores:
                store = pltpu.make_async_copy(source, target, out_sems.at[len(begun)])
                store.start()
                begun.append(store)
        for store in begun:
            store.wait()

    @pl.when(section == 0)
    def _():
        run(0, 1)

    @pl.when(section == 1)
    def _():
        run(1, 0)


def place(pieces, where, widths=None):
    rows, columns = pieces[0].shape[1:]
    kind = pieces[0].dtype
    widths = widths or (columns,)
    shapes = [jax.ShapeDtypeStruct((4, 4, rows, width), kind) for width in widths] * 2
    return pl.pallas_call(
        functools.partial(place_kernel, widths),
        out_shape=shapes,
        in_specs=[pl.BlockSpec(memory_space=pltpu.SMEM)]
        + [pl.BlockSpec(memory_space=pl.ANY)] * len(pieces),
        out_specs=[pl.BlockSpec(memory_space=pl.ANY)] * len(shapes),
        scratch_shapes=[
            pltpu.VMEM((32, rows, columns), kind),
            pltpu.SemaphoreType.DMA((32,)),
            pltpu.SemaphoreType.DMA((32 * len(widths),)),
        ],
        compiler_params=pltpu.CompilerParams(vmem_limit_bytes=32 * 1024 * 1024),
        cost_estimate=SHORT,
    )(where, *pieces)


def add_low(first, second):
    return (first.astype(jnp.float32) + second.astype(jnp.float32)).astype(jnp.bfloat16)


def pick(array, index, axis):
    return lax.dynamic_index_in_dim(array, index, axis, keepdims=False)


def local_call(kernel, where, arrays, outs, scratch=(), steps=1, kind=jnp.bfloat16):
    def spec(shape, first):
        if first is None:
            return pl.BlockSpec(shape, lambda i: (0,) * len(shape))
        block = (1, *shape[1:])
        return pl.BlockSpec(block, lambda i: (first + i,) + (0,) * (len(shape) - 1))

    pairs = [item if isinstance(item, tuple) else (item, None) for item in arrays]
    return pl.pallas_call(
        kernel,
        grid=(steps,),
        out_shape=[jax.ShapeDtypeStruct(shape, kind) for shape in outs],
        in_specs=[pl.BlockSpec(memory_space=pltpu.SMEM)]
        + [spec(array.shape, first) for array, first in pairs],
        out_specs=[spec(shape, None if steps == 1 else 0) for shape in outs],
        scratch_shapes=list(scratch),
        compiler_params=pltpu.CompilerParams(vmem_limit_bytes=48 * 1024 * 1024),
        cost_estimate=SHORT,
    )(where, *(array for array, _ in pairs))


def across_kernel(where_ref, own, got, own_high, got_high, *outs):
    low_keep, low_send, high_keep, high_send = outs
    section, side = where_ref[0], where_ref[2]
    rows, half = low_keep.shape[2:]

    def total(first, second, to_side, start, width):
        place = (
            0,
            pl.ds(pl.multiple_of(to_side * rows, 16), rows),
            pl.ds(pl.multiple_of(start, 128), width),
        )
        return add_low(first[place], second[place])

    for to_side in range(2):
        low_keep[0, to_side] = total(own, got, to_side, section * half, half)
        low_send[0, to_side] = total(own, got, to_side, (1 - section) * half, half)
    high_keep[0] = total(own_high, got_high, side, 0, 2 * half)
    high_send[0] = total(own_high, got_high, 1 - side, 0, 2 * half)


def along_kernel(
    where_ref, low, high, low_got, high_got, low_keep, low_send, high_keep, high_send
):
    section, side = where_ref[0], where_ref[2]
    half = low_keep.shape[2]
    for to_side, target in ((side, low_keep), (1 - side, low_send)):
        target[0] = add_low(low[0, to_side], low_got[0, to_side])
    for to_section, target in ((section, high_keep), (1 - section, high_send)):
        columns = pl.ds(pl.multiple_of(to_section * half, 128), half)
        target[0] = add_low(high[0, :, columns], high_got[0, :, columns])


def shards_kernel(where_ref, low, high, low_got, high_got, own, *rest):
    sends, both = rest[:3], rest[3]
    here = where_ref[3]
    for shard in range(2):
        both[shard] = add_low(low[shard], low_got[shard])
        both[2 + shard] = add_low(high[shard], high_got[shard])
    own[...] = both[here]
    for i, target in enumerate(sends):
        target[...] = both[lax.rem(here + 3 - i, 4)]


def back_kernel(where_ref, *refs):
    keep, give = refs[-2:]

    def put(first, second):
        start = 0
        for member in range(len(refs) // 8):
            width = refs[member * 8].shape[1]
            for block, target in enumerate((first, second)):
                terms = refs[member * 8 + block * 4 : member * 8 + block * 4 + 4]
                total = sum(term[...].astype(jnp.float32) for term in terms)
                target[:, start : start + width] = total.astype(jnp.bfloat16)
            start += width

    @pl.when(where_ref[0] == 0)
    def _():
        put(keep, give)

    @pl.when(where_ref[0] == 1)
    def _():
        put(give, keep)


def grad_kernel(kinds, where_ref, *refs):
    count = len(kinds)
    lefts, rights = refs[:count], refs[count : 2 * count]
    own, send, sums, total = refs[2 * count :]
    core = where_ref[1]
    step = pl.program_id(0)

    def run(left, right):
        total[...] = contract_rows(left[...], right[...])
        sums[...] = jnp.sum(right[...].astype(jnp.float32), axis=0, keepdims=True)
        parts, rows = own.shape[:2]
        for part in range(parts):
            for to_core, target in ((core, own), (1 - core, send)):
                start = pl.multiple_of((2 * part + to_core) * rows, 32)
                target[part] = total[pl.ds(start, rows), :].astype(jnp.bfloat16)

    first = 0
    for kind, left, right in zip(kinds, lefts, rights):

        @pl.when((step >= first) & (step < first + kind))
        def _(left=left, right=right):
            run(left, right)

        first += kind


def grad_call(where, pairs, deep=False):
    width = 768
    row_count = pairs[0][0].shape[0]
    lefts, rights = [left for left, _ in pairs], [right for _, right in pairs]
    kinds = [max(left.shape[1], right.shape[1]) // width for left, right in pairs]
    steps = sum(kinds)
    firsts = [sum(kinds[:index]) for index in range(len(kinds))]

    def spec(wide, first, kind):
        if not wide:
            return pl.BlockSpec((row_count, width), lambda j: (0, 0))
        return pl.BlockSpec((row_count, width), lambda j: (0, jnp.clip(j - first, 0, kind - 1)))

    in_specs = [pl.BlockSpec(memory_space=pltpu.SMEM)]
    for arrays in (lefts, rights):
        for array, first, kind in zip(arrays, firsts, kinds):
            in_specs.append(spec(array.shape[1] > width, first, kind))
    if deep:
        shape, block = (4, lefts[0].shape[1] // 8, width), (1, lefts[0].shape[1] // 8, width)
        out_spec = pl.BlockSpec(block, lambda j: (j, 0, 0))
        sums_shape, sums_spec = (1, width), pl.BlockSpec((1, width), lambda j: (0, 0))
    else:
        shape, block = (4, width // 8, steps * width), (4, width // 8, width)
        out_spec = pl.BlockSpec(block, lambda j: (0, 0, j))
        sums_shape, sums_spec = (1, steps * width), pl.BlockSpec((1, width), lambda j: (0, j))
    return pl.pallas_call(
        functools.partial(grad_kernel, kinds),
        grid=(steps,),
        out_shape=[jax.ShapeDtypeStruct(shape, jnp.bfloat16)] * 2
        + [jax.ShapeDtypeStruct(sums_shape, jnp.float32)],
        in_specs=in_specs,
        out_specs=[out_spec, out_spec, sums_spec],
        scratch_shapes=[pltpu.VMEM((width, width), jnp.float32)],
        compiler_params=pltpu.CompilerParams(vmem_limit_bytes=40 * 1024 * 1024),
        cost_estimate=SHORT,
    )(where, *lefts, *rights)


GELU_SCALE = 0.7978845608028654
GELU_CUBE = 0.044715


def expand_kernel(normed_ref, weight_ref, bias_ref, active_ref, slope_ref):
    values = jnp.dot(normed_ref[...], weight_ref[...], preferred_element_type=jnp.float32)
    values = values + bias_ref[...]
    square = values * values
    bent = jnp.tanh(GELU_SCALE * values * (1.0 + GELU_CUBE * square))
    half = 0.5 * (1.0 + bent)
    active_ref[...] = (values * half).astype(jnp.bfloat16)
    inner = GELU_SCALE * (1.0 + 3.0 * GELU_CUBE * square)
    slope_ref[...] = (half + 0.5 * values * (1.0 - bent * bent) * inner).astype(jnp.bfloat16)


def expand_call(normed, weight, bias):
    row_count, depth = normed.shape
    columns = weight.shape[1]
    width = depth
    out_spec = pl.BlockSpec((row_count, width), lambda j: (0, j))
    return pl.pallas_call(
        expand_kernel,
        grid=(columns // width,),
        out_shape=[jax.ShapeDtypeStruct((row_count, columns), jnp.bfloat16)] * 2,
        in_specs=[
            pl.BlockSpec((row_count, depth), lambda j: (0, 0)),
            pl.BlockSpec((depth, width), lambda j: (0, j)),
            pl.BlockSpec((1, width), lambda j: (0, j)),
        ],
        out_specs=[out_spec, out_spec],
        compiler_params=pltpu.CompilerParams(vmem_limit_bytes=40 * 1024 * 1024),
        cost_estimate=SHORT,
    )(normed, weight, bias[None])


def ordered(own, other, index, axis):
    first = jnp.where(index == 0, own, other)
    second = jnp.where(index == 0, other, own)
    return jnp.concatenate([first, second], axis=axis)


class Moves:
    def __init__(self, where):
        self.where = where

    over_x = staticmethod(lambda array: swap(array, "section", 1))
    over_y = staticmethod(lambda array: swap(array, "replica", 2))
    to_mate = staticmethod(lambda array: swap(array, "replica", 1))

    def gather(self):
        def along(own):
            return ((), [(own, lambda array: lax.all_gather(array, "shard", axis=0))])

        along.late = 1

        def across(chunks):
            return ((chunks,), [(chunks, self.over_x), (chunks, self.over_y)])

        def beyond(*arrays):
            _, over_x, over_y = arrays
            return (arrays, [(over_x[:2], self.over_y), (over_y[2:], self.over_x)])

        return [along, across, beyond]

    def laid(self, state, widths=None):
        mine = jnp.concatenate(state, axis=0)
        return place((mine, self.to_mate(mine)), self.where, widths)

    def reduce(self):
        def mates(own, send):
            return ((own,), [(send, self.to_mate)])

        def across(own, got):
            shards, rows, columns = own.shape
            low = (2, 2, rows // 2, columns // 2)
            high = (2, rows // 2, columns)
            result = local_call(
                across_kernel,
                self.where,
                ((own, 0), (got, 0), (own, 2), (got, 2)),
                (low, low, high, high),
                steps=2,
            )
            low_keep, low_send, high_keep, high_send = result
            return ((low_keep, high_keep), [(low_send, self.over_x), (high_send, self.over_y)])

        def along(*state):
            shape = (2, *state[0].shape[2:])
            result = local_call(
                along_kernel, self.where, [(array, 0) for array in state], (shape,) * 4, steps=2
            )
            low_keep, low_send, high_keep, high_send = result
            return ((low_keep, high_keep), [(low_send, self.over_y), (high_send, self.over_x)])

        def shards(*state):
            shape = state[0].shape[1:]
            scratch = [pltpu.VMEM((4, *shape), jnp.bfloat16)]
            result = local_call(shards_kernel, self.where, state, (shape,) * 4, scratch)
            turns = [functools.partial(turn, axis="shard", step=i) for i in (1, 2, 3)]
            return ((result[0],), list(zip(result[1:], turns)))

        return [mates, across, along, shards]

    def spread(self):
        def back(*pairs):
            terms = [term for pair in pairs for state in pair for term in state]
            rows = terms[0].shape[0]
            shape = (rows, sum(pair[0][0].shape[1] for pair in pairs))
            keep, give = local_call(back_kernel, self.where, terms, (shape, shape))
            return ((keep,), [(give, self.over_x)])

        def around(keep, got):
            rows = jnp.stack([keep, got])

            def corner(array):
                over_y = self.over_y(array)
                return (over_y, self.to_mate(over_y))

            return ((rows,), [(rows, self.to_mate), (rows, corner)])

        return [back, around]

    @staticmethod
    def exchange(late):
        def step(section, first, second):
            give = jnp.where(section == 0, second, first)
            if not late:
                return ((), [(give, Moves.over_x)])
            return ((), [(give, lambda array: lax.all_gather(array, "section", axis=0))])

        step.late = late
        return [step]

    @staticmethod
    def total():
        def step_of(axis, bit):
            def step(*terms):
                array = sum(terms[1:], terms[0])
                return ((array,), [(array, lambda array: swap(array, axis, bit))])

            return step

        pairs = (("replica", 1), ("section", 1), ("replica", 2), ("shard", 1), ("shard", 2))
        return [step_of(*pair) for pair in pairs]


class Flows:
    def __init__(self):
        self.left = {}
        self.states = {}
        self.open = {}

    def start(self, name, steps, *state):
        self.left[name] = list(steps)
        self.states[name] = state

    def extend(self, name, steps):
        self.left[name] += steps

    def stage(self, compute=lambda: (), *inputs):
        names = [name for name in self.left if self.left[name]]
        steps = [self.left[name].pop(0) for name in names]
        states = [self.states[name] for name in names]
        inputs, states = lax.optimization_barrier((inputs, states))
        ready = [step(*state) for step, state in zip(steps, states)]
        kept = [keep for keep, _ in ready]
        sent = [[array for array, _ in sends] for _, sends in ready]
        inputs, kept, sent = lax.optimization_barrier((inputs, kept, sent))
        got = [
            [move(array) for array, (_, move) in zip(arrays, sends)]
            for arrays, (_, sends) in zip(sent, ready)
        ]
        late = [getattr(step, "late", 0) for step in steps]
        waited = [result for result, slow in zip(got, late) if not slow]
        due = [name for name in self.open if self.open[name] == 1]
        closing = [self.states[name] for name in due]
        results, waited, closing = lax.optimization_barrier((compute(*inputs), waited, closing))
        self.states.update(zip(due, closing))
        self.open = {name: left - 1 for name, left in self.open.items() if left > 1}
        self.open.update({name: slow for name, slow in zip(names, late) if slow})
        waited = iter(waited)
        for name, keep, result, slow in zip(names, kept, got, late):
            self.states[name] = (*keep, *(result if slow else next(waited)))
        return results


def close_kernel(where_ref, *refs):
    section, core, side = (where_ref[i] for i in range(3))
    wide_pieces, last_pieces = refs[:4], refs[4:8]
    input_out, expand_out, output_out, contract_out = refs[8:]
    input_half = input_out.shape[1] // 2
    contract_half = contract_out.shape[1] // 2
    split = expand_out.shape[1] - (wide_pieces[0].shape[2] - input_half)

    def one(far_core, far_side, far_section):
        at_section = section if far_section == 0 else 1 - section
        at_side = side if far_side == 0 else 1 - side
        at_core = core if far_core == 0 else 1 - core
        rank = at_core * 2 + at_side
        wide = wide_pieces[far_core * 2 + far_side][far_section].astype(jnp.float32)
        rows = pl.ds(pl.multiple_of(rank * wide.shape[0], 16), wide.shape[0])
        columns = pl.ds(pl.multiple_of(at_section * input_half, 128), input_half)
        input_out[rows, columns] = wide[:, :input_half]
        wide = wide[:, input_half:]

        @pl.when(at_section == 0)
        def _():
            expand_out[rows, : wide.shape[1]] = wide

        @pl.when(at_section == 1)
        def _():
            expand_out[rows, wide.shape[1] :] = wide[:, :split]
            output_out[rows, :] = wide[:, split:]

        last = last_pieces[far_core * 2 + far_side][far_section].astype(jnp.float32)
        rows = pl.ds(pl.multiple_of(rank * last.shape[0], 16), last.shape[0])
        columns = pl.ds(pl.multiple_of(at_section * contract_half, 128), contract_half)
        contract_out[rows, columns] = last

    for far_core in range(2):
        for far_side in range(2):
            for far_section in range(2):
                one(far_core, far_side, far_section)


def close(where, wide, contract, shapes):
    def pieces(state):
        own, mate, (over_y, mate_y) = state
        return (own, over_y, mate, mate_y)

    arrays = (*pieces(wide), *pieces(contract))
    return local_call(close_kernel, where, arrays, shapes, kind=jnp.float32)

VECTORS = ("gain_a", "shift_a", "bias_q", "bias_v", "bias_o", "gain_f", "shift_f", "bias_c")


def forward_attention(params, hidden_low, segment):
    hidden = hidden_low.astype(jnp.float32)
    normed = layer_norm(hidden, params["gain_a"], params["shift_a"]).astype(jnp.bfloat16)
    zeros = jnp.zeros_like(params["bias_q"])
    joint_bias = jnp.concatenate([params["bias_q"], zeros, params["bias_v"]])
    joint_low = (
        jnp.dot(normed, params["input"], preferred_element_type=jnp.float32) + joint_bias
    ).astype(jnp.bfloat16)
    mixed_low, log_sums = attend_forward(joint_low, segment)
    middle = (
        hidden
        + jnp.dot(mixed_low, params["output"], preferred_element_type=jnp.float32)
        + params["bias_o"]
    )
    return dict(
        hidden_low=hidden_low,
        normed=normed,
        joint_low=joint_low,
        log_sums=log_sums,
        mixed_low=mixed_low,
        middle=middle,
    )


def forward_expand(params, middle):
    normed_two = layer_norm(middle, params["gain_f"], params["shift_f"]).astype(jnp.bfloat16)
    activated, slope = expand_call(normed_two, params["expand"], params["bias_e"])
    return dict(normed_two=normed_two, slope=slope, activated=activated)


def forward_contract(params, middle, activated, living):
    result = (
        middle
        + jnp.dot(activated, params["contract"], preferred_element_type=jnp.float32)
        + params["bias_c"]
    )
    return (result * living[:, None]).astype(jnp.bfloat16)


class Backward:
    def __init__(self, params, kept, segment, living, where, upstream):
        self.params, self.segment, self.living, self.where = params, segment, living, where
        self.held = dict(kept, upstream=upstream)

    def run(self, flow, part):
        function, names = {
            "expand": (self.expand, ("upstream", "activated", "slope")),
            "norm": (
                self.norm,
                ("expand_low", "normed_two", "out_grad", "middle", "mixed_low"),
            ),
            "attention": (self.attention, ("joint_low", "log_sums", "mixed_grad")),
            "input": (self.input, ("normed", "joint_grad")),
            "last": (self.last, ("joint_grad", "middle_grad", "hidden_low")),
            "both": (self.both, ("normed", "joint_grad", "middle_grad", "hidden_low")),
        }[part]
        self.held.update(flow.stage(function, *(self.held[name] for name in names)))

    def grads(self, name, *pairs, deep=False):
        if self.where is not None:
            own, send, sums = grad_call(self.where, pairs, deep)
            return {name + "_own": own, name + "_send": send, name + "_sums": sums[0]}
        whole = jnp.concatenate([contract_rows(*pair).astype(jnp.bfloat16) for pair in pairs], axis=1)
        sums = [jnp.sum(right.astype(jnp.float32), axis=0) for _, right in pairs]
        return {name + "_own": whole, name + "_sums": jnp.concatenate(sums)}

    def expand(self, upstream, activated, slope):
        out_grad = upstream.astype(jnp.float32) * self.living[:, None]
        low = out_grad.astype(jnp.bfloat16)
        found = self.grads("contract", (activated, low), deep=True)
        activated_grad = times_transpose(low, self.params["contract"])
        expand_low = (activated_grad * slope.astype(jnp.float32)).astype(jnp.bfloat16)
        return dict(found, out_grad=out_grad, expand_low=expand_low)

    def norm(self, expand_low, normed_two, out_grad, middle, mixed_low):
        normed_grad = times_transpose(expand_low, self.params["expand"])
        _, pull = jax.vjp(layer_norm, middle, self.params["gain_f"], self.params["shift_f"])
        norm_grad, gain_grad, shift_grad = pull(normed_grad)
        middle_grad = out_grad + norm_grad
        branch_low = middle_grad.astype(jnp.bfloat16)
        mixed_grad = times_transpose(branch_low, self.params["output"]).astype(jnp.bfloat16)
        found = self.grads("expand", (normed_two, expand_low), (mixed_low, branch_low))
        return dict(
            found, middle_grad=middle_grad, mixed_grad=mixed_grad, gain_f=gain_grad, shift_f=shift_grad
        )

    def attention(self, joint_low, log_sums, mixed_grad):
        return dict(joint_grad=attend_backward(joint_low, log_sums, mixed_grad, self.segment))

    def input(self, normed, joint_grad):
        return self.grads("input", (normed, joint_grad))

    def last(self, joint_grad, middle_grad, hidden_low):
        normed_grad = times_transpose(joint_grad, self.params["input"])
        _, pull = jax.vjp(
            layer_norm,
            hidden_low.astype(jnp.float32),
            self.params["gain_a"],
            self.params["shift_a"],
        )
        norm_grad, gain_grad, shift_grad = pull(normed_grad)
        grad = middle_grad + norm_grad
        return dict(grad_low=grad.astype(jnp.bfloat16), gain_a=gain_grad, shift_a=shift_grad)

    def both(self, normed, joint_grad, middle_grad, hidden_low):
        found = self.input(normed, joint_grad)
        return dict(found, **self.last(joint_grad, middle_grad, hidden_low))

    def small(self):
        held = self.held
        width = held["gain_a"].shape[0]
        split = held["expand_sums"].shape[0] - width
        held = dict(
            held,
            bias_q=held["input_sums"][:width],
            bias_v=held["input_sums"][2 * width :],
            bias_o=held["expand_sums"][split:],
            bias_c=held["contract_sums"],
        )
        vectors = [held[name] for name in VECTORS] + [held["expand_sums"][:split]]
        return jnp.concatenate(vectors).reshape(-1, width)


def per_device(
    tokens,
    cotangent,
    lengths,
    assignment,
    attention_gain,
    attention_shift,
    input_weight,
    query_bias,
    value_bias,
    output_weight,
    output_bias,
    feedforward_gain,
    feedforward_shift,
    expand_weight,
    expand_bias,
    contract_weight,
    contract_bias,
):
    section = lax.axis_index("section")
    shard = lax.axis_index("shard")
    replica = lax.axis_index("replica")
    shards, replicas = lax.axis_size("shard"), lax.axis_size("replica")
    core, side = replica % 2, replica // 2
    model_width = tokens.shape[1]
    cube = shards == 4 and replicas == 4
    where = jnp.stack([section, core, side, shard]).astype(jnp.int32)

    slot = (shard * replicas + replica) * MICRO + section
    matches = (assignment == slot).astype(jnp.int32)
    counts = jnp.sum(matches[:, None] * lengths, axis=0, dtype=jnp.int32)
    segment, living = slot_layout(counts, ROWS)
    entering = lax.dynamic_slice_in_dim(tokens, section * ROWS, ROWS, 0)
    seed = lax.dynamic_slice_in_dim(cotangent, section * ROWS, ROWS, 0)

    vectors = (
        attention_gain,
        attention_shift,
        query_bias,
        value_bias,
        output_bias,
        feedforward_gain,
        feedforward_shift,
        contract_bias,
        expand_bias,
    )
    small_own = jnp.concatenate(vectors, axis=1)
    expand_width = expand_weight.shape[2]
    flow = Flows()
    moves = Moves(where)

    def joined(members):
        return [member.reshape(-1, member.shape[-1]) for member in members]

    def named(small_all, **pairs):
        count = len(VECTORS)
        split = small_all.shape[2] - expand_bias.shape[1]
        lines = small_all[:, :, :split].reshape(2, shards, count, split // count)
        lines = lines.transpose(0, 2, 1, 3).reshape(2, count, model_width).astype(jnp.float32)
        bias_e = small_all[:, :, split:].reshape(2, expand_width).astype(jnp.float32)
        found = []
        for block in range(2):
            params = {name: lines[block, index] for index, name in enumerate(VECTORS)}
            params["bias_e"] = bias_e[block]
            params.update({name: pair[block] for name, pair in pairs.items()})
            found.append(params)
        return found

    if cube:

        def chunk(weight):
            size = weight.shape[1] // 4
            return lax.dynamic_slice_in_dim(weight[0], (core * 2 + side) * size, size, 0)

        input_chunk, output_chunk = chunk(input_weight), chunk(output_weight)
        small_rows = small_own.shape[1] // 128
        short = input_chunk.shape[0] - small_rows
        padded = jnp.pad(small_own.reshape(small_rows, 128), ((0, short), (0, 0)))
        opening = jnp.concatenate([input_chunk, output_chunk, padded], axis=1)
        widths = (input_chunk.shape[1], output_chunk.shape[1], 128)
        flow.start("gather_open", moves.gather(), opening)
        flow.stage()
        flow.start("gather_expand", moves.gather(), chunk(expand_weight))
        flow.stage()
        flow.start("gather_contract", moves.gather(), chunk(contract_weight))
        flow.stage()

        def open_part(state, hidden_low):
            laid = moves.laid(state, widths)
            small_all = jnp.stack(laid[2::3])[:, :, 0, :small_rows].reshape(2, shards, -1)
            found = named(small_all, input=joined(laid[0::3]), output=joined(laid[1::3]))
            return (found, forward_attention(found[0], hidden_low, segment))

        (params, kept_first) = flow.stage(open_part, flow.states["gather_open"], entering)

        def middle_part(state, middle):
            expand_all = joined(moves.laid(state))
            held = forward_expand(dict(params[0], expand=expand_all[0]), middle)
            return (expand_all, held)

        expand_all, held = flow.stage(
            middle_part, flow.states["gather_expand"], kept_first["middle"]
        )
        kept_first.update(held)
        contract_all = joined(moves.laid(flow.states["gather_contract"]))
        for block in range(2):
            params[block].update(expand=expand_all[block], contract=contract_all[block])
    else:

        def whole(weight):
            held = lax.all_gather(weight, "shard", axis=1, tiled=True)
            return lax.all_gather(held, "section", axis=0, tiled=True)

        params = named(
            whole(small_own[None]),
            input=whole(input_weight),
            output=whole(output_weight),
            expand=whole(expand_weight),
            contract=whole(contract_weight),
        )
        kept_first = forward_attention(params[0], entering, segment)
        kept_first.update(forward_expand(params[0], kept_first["middle"]))

    middle_out = forward_contract(
        params[0], kept_first["middle"], kept_first["activated"], living
    )

    def second_forward(hidden_low):
        kept = forward_attention(params[1], hidden_low, segment)
        kept.update(forward_expand(params[1], kept["middle"]))
        return (kept, forward_contract(params[1], kept["middle"], kept["activated"], living))

    kept_second, last_out = second_forward(middle_out)

    def begin(block, name):
        tag = ("first_" if block is first else "second_") + name
        if cube:
            flow.start(tag, moves.reduce(), block.held[name + "_own"], block.held[name + "_send"])

    def spread(name, *members):
        if cube:
            pairs = [(flow.states["first_" + m], flow.states["second_" + m]) for m in members]
            flow.start(name, moves.spread(), *pairs)

    first = None
    second = Backward(params[1], kept_second, segment, living, where if cube else None, seed)
    flow.start("out", moves.exchange(0), section, middle_out, last_out)
    second.run(flow, "expand")
    begin(second, "contract")
    second.run(flow, "norm")
    begin(second, "expand")
    second.run(flow, "attention")
    second.run(flow, "both")
    begin(second, "input")

    first = Backward(params[0], kept_first, segment, living, where if cube else None, second.held["grad_low"])
    first.run(flow, "expand")
    begin(first, "contract")
    first.run(flow, "norm")
    begin(first, "expand")
    first.run(flow, "attention")
    first.run(flow, "input")
    begin(first, "input")
    first.run(flow, "last")
    small_both = jnp.stack([first.small(), second.small()])
    flow.start("small", moves.total() if cube else [], small_both)
    flow.start("grad", moves.exchange(4), section, first.held["grad_low"], second.held["grad_low"])
    flow.stage()
    flow.stage()
    flow.stage()
    spread("wide", "input", "expand")
    spread("contract", "contract")
    flow.stage()
    flow.stage()

    def own_block(name, first_value, second_value):
        keep = jnp.where(section == 0, first_value, second_value)
        got = flow.states[name][0]
        got = pick(got, 1 - section, 0) if got.ndim == 3 else got
        return ordered(keep, got, section, 0)

    block_out = own_block("out", middle_out, last_out)
    grad_out = own_block("grad", first.held["grad_low"], second.held["grad_low"])
    grad_out = grad_out.astype(jnp.float32)

    if cube:
        small_sum = flow.states["small"][0] + flow.states["small"][1]
        shapes = [
            weight.shape[1:] for weight in (input_weight, expand_weight, output_weight, contract_weight)
        ]
        large = close(where, flow.states["wide"], flow.states["contract"], shapes)
    else:
        small_sum = lax.psum(small_both, ("section", "shard", "replica"))
        large = []
        for name in ("input_own", "expand_own", "contract_own"):
            wide = jnp.stack([block.held[name] for block in (first, second)])
            held = lax.psum_scatter(wide, "section", scatter_dimension=0, tiled=True)
            held = lax.psum_scatter(held[0], "shard", scatter_dimension=0, tiled=True)
            large.append(lax.psum(held, "replica").astype(jnp.float32))
        large[1:2] = [large[1][:, :expand_width], large[1][:, expand_width:]]
    small_sum = pick(small_sum, section, 0)
    lines = small_sum[: len(VECTORS)].reshape(len(VECTORS), shards, -1)
    lines = pick(lines, shard, 1)
    small = {name: lines[index][None] for index, name in enumerate(VECTORS)}
    bias_e_grad = pick(small_sum[len(VECTORS) :].reshape(shards, -1), shard, 0)[None]
    input_grad, expand_grad, output_grad, contract_grad = (member[None] for member in large)
    return (
        block_out[None],
        grad_out[None],
        small["gain_a"],
        small["shift_a"],
        input_grad,
        small["bias_q"],
        small["bias_v"],
        output_grad,
        small["bias_o"],
        small["gain_f"],
        small["shift_f"],
        expand_grad,
        bias_e_grad,
        contract_grad,
        small["bias_c"],
    )


def solution(mesh):
    placed = (
        P(("shard", "replica"), None),
        P(("shard", "replica"), None),
        P(),
        P(),
        P("section", "shard"),
        P("section", "shard"),
        P("section", "shard", None),
        P("section", "shard"),
        P("section", "shard"),
        P("section", "shard", None),
        P("section", "shard"),
        P("section", "shard"),
        P("section", "shard"),
        P("section", "shard", None),
        P("section", "shard"),
        P("section", "shard", None),
        P("section", "shard"),
    )
    return jax.shard_map(
        per_device,
        mesh=mesh,
        in_specs=placed,
        out_specs=(
            P("section", ("shard", "replica"), None),
            P("section", ("shard", "replica"), None),
            P("section", "shard"),
            P("section", "shard"),
            P("section", "shard", None),
            P("section", "shard"),
            P("section", "shard"),
            P("section", "shard", None),
            P("section", "shard"),
            P("section", "shard"),
            P("section", "shard"),
            P("section", "shard", None),
            P("section", "shard"),
            P("section", "shard", None),
            P("section", "shard"),
        ),
        check_vma=False,
    )
```

```python
import functools

import jax
import jax.numpy as jnp
from jax import lax
from jax.experimental import pallas as pl
from jax.experimental.pallas import tpu as pltpu
from jax.sharding import PartitionSpec as P

HEADS = 12
ROWS = 512
MICRO = 2


EPSILON = 1e-05
MASKED_SCORE = -1e30

SHORT = pl.CostEstimate(flops=1, bytes_accessed=1, transcendentals=0)


def layer_norm(hidden, norm_gain, norm_shift):
    mean = jnp.mean(hidden, axis=-1, keepdims=True)
    center = hidden - mean
    spread = jnp.mean(center * center, axis=-1, keepdims=True)
    scale = lax.rsqrt(spread + EPSILON)
    return (center * scale * norm_gain + norm_shift, (mean, scale))


def layer_norm_back(hidden, stats, norm_gain, grad):
    mean, scale = stats
    hat = (hidden - mean) * scale
    scaled = grad * norm_gain
    first = jnp.mean(scaled, axis=-1, keepdims=True)
    second = jnp.mean(scaled * hat, axis=-1, keepdims=True)
    hidden_grad = scale * (scaled - first - hat * second)
    return (hidden_grad, jnp.sum(grad * hat, axis=0), jnp.sum(grad, axis=0))


def slot_layout(counts, row_count):
    bounds = jnp.cumsum(counts, dtype=jnp.int32)
    places = jnp.arange(row_count, dtype=jnp.int32)
    segment = jnp.sum(
        (bounds[None, :] <= places[:, None]).astype(jnp.int32), axis=1, dtype=jnp.int32
    )
    living = (places < bounds[-1]).astype(jnp.float32)
    return (segment, living)


def gelu_tanh(values):
    return jax.nn.gelu(values, approximate=True)


def contract_rows(left_side, right_side):
    return lax.dot_general(
        left_side, right_side, (((0,), (0,)), ((), ())), preferred_element_type=jnp.float32
    )


def times_transpose(left_side, right_side):
    return lax.dot_general(
        left_side, right_side, (((1,), (1,)), ((), ())), preferred_element_type=jnp.float32
    )


def masked_bias(segment_column, segment_row):
    row_count = segment_column.shape[0]
    query_places = lax.broadcasted_iota(jnp.int32, (row_count, row_count), 0)
    key_places = lax.broadcasted_iota(jnp.int32, (row_count, row_count), 1)
    allowed = (segment_column == segment_row) & (key_places <= query_places)
    return jnp.where(allowed, 0.0, MASKED_SCORE)


def head_lanes(block, head):
    half = block.shape[1] // 2
    lanes = lax.broadcasted_iota(jnp.int32, block.shape, 1)
    return jnp.where((lanes < half) == (head == 0), block, jnp.zeros_like(block))


def attend_kernel(column_ref, row_ref, q_ref, k_ref, v_ref, mixed_ref, log_ref, bias_ref):
    @pl.when(pl.program_id(0) == 0)
    def _():
        bias_ref[...] = masked_bias(column_ref[...], row_ref[...])

    row_count, width = q_ref.shape
    tall = row_count // 2
    scale = (width // 2) ** (-0.5)
    first_lanes = lax.broadcasted_iota(jnp.int32, (tall, width), 1) < width // 2
    for start in (0, tall):
        stop = start + tall
        queries = q_ref[start:stop] * jnp.asarray(scale, q_ref.dtype)
        outs, logs = [], []
        for head in range(2):
            scores = times_transpose(head_lanes(queries, head), k_ref[:stop])
            scores = scores + bias_ref[start:stop, :stop]
            row_max = jnp.max(scores, axis=1, keepdims=True)
            exponent = jnp.exp(scores - row_max)
            row_total = jnp.sum(exponent, axis=1, keepdims=True)
            probs = (exponent * (1.0 / row_total)).astype(jnp.bfloat16)
            outs.append(jnp.dot(probs, v_ref[:stop], preferred_element_type=jnp.float32))
            logs.append(jnp.broadcast_to(row_max + jnp.log(row_total), (tall, width)))
        mixed_ref[start:stop] = jnp.where(first_lanes, *outs).astype(jnp.bfloat16)
        log_ref[start:stop] = jnp.where(first_lanes, *logs)


def attend_back_kernel(
    column_ref, row_ref, q_ref, k_ref, v_ref, grad_ref, log_ref, dq_ref, dk_ref, dv_ref, bias_ref
):
    @pl.when(pl.program_id(0) == 0)
    def _():
        bias_ref[...] = masked_bias(column_ref[...], row_ref[...])

    row_count, width = q_ref.shape
    tall = row_count // 2
    scale = (width // 2) ** (-0.5)
    first_lanes = lax.broadcasted_iota(jnp.int32, (tall, width), 1) < width // 2
    key_parts, value_parts = [], []
    for start in (0, tall):
        stop = start + tall
        queries = q_ref[start:stop] * jnp.asarray(scale, q_ref.dtype)
        query_parts = []
        key_grad = value_grad = 0.0
        for head in range(2):
            mine = head_lanes(queries, head)
            grad = head_lanes(grad_ref[start:stop], head)
            lane = head * (width // 2)
            scores = times_transpose(mine, k_ref[:stop]) + bias_ref[start:stop, :stop]
            probs = jnp.exp(scores - log_ref[start:stop, lane : lane + 1])
            prob_grad = times_transpose(grad, v_ref[:stop])
            center = jnp.sum(prob_grad * probs, axis=1, keepdims=True)
            score_grad = (probs * (prob_grad - center)).astype(jnp.bfloat16)
            query_parts.append(
                jnp.dot(score_grad, k_ref[:stop], preferred_element_type=jnp.float32)
            )
            key_grad = key_grad + contract_rows(score_grad, mine)
            value_grad = value_grad + contract_rows(probs.astype(jnp.bfloat16), grad)
        dq_ref[start:stop] = (jnp.where(first_lanes, *query_parts) * scale).astype(jnp.bfloat16)
        key_parts.append(key_grad)
        value_parts.append(value_grad)
    for parts, target in ((key_parts, dk_ref), (value_parts, dv_ref)):
        target[:tall] = (parts[0] + parts[1][:tall]).astype(jnp.bfloat16)
        target[tall:] = parts[1][tall:].astype(jnp.bfloat16)


def attention_call(kernel, segment, blocks, outs):
    row_count = segment.shape[0]
    pairs = HEADS // 2
    model_width = blocks[0][0].shape[1] // 3
    lanes = model_width // pairs

    def spec(first):
        return pl.BlockSpec((row_count, lanes), lambda pair: (0, first + pair))

    return pl.pallas_call(
        kernel,
        grid=(pairs,),
        out_shape=[jax.ShapeDtypeStruct((row_count, model_width), kind) for kind in outs],
        in_specs=[
            pl.BlockSpec((row_count, 1), lambda pair: (0, 0)),
            pl.BlockSpec((1, row_count), lambda pair: (0, 0)),
        ]
        + [spec(first) for _, first in blocks],
        out_specs=[spec(0) for _ in outs],
        scratch_shapes=[pltpu.VMEM((row_count, row_count), jnp.float32)],
        compiler_params=pltpu.CompilerParams(vmem_limit_bytes=20 * 1024 * 1024),
        cost_estimate=SHORT,
    )(segment[:, None], segment[None, :], *(array for array, _ in blocks))


def attend_forward(joint_low, segment):
    pairs = HEADS // 2
    blocks = [(joint_low, first * pairs) for first in range(3)]
    return attention_call(attend_kernel, segment, blocks, (jnp.bfloat16, jnp.float32))


def attend_backward(joint_low, log_sums, mixed_grad, segment):
    pairs = HEADS // 2
    blocks = [(joint_low, first * pairs) for first in range(3)]
    blocks += [(mixed_grad, 0), (log_sums, 0)]
    parts = attention_call(attend_back_kernel, segment, blocks, (jnp.bfloat16,) * 3)
    return jnp.concatenate(parts, axis=1)


def swap(block, axis, bit):
    return lax.ppermute(block, axis, [(i, i ^ bit) for i in range(lax.axis_size(axis))])


def turn(block, axis, step):
    size = lax.axis_size(axis)
    return lax.ppermute(block, axis, [((i + step) % size, i) for i in range(size)])


def one_way(block, axis, source, target):
    return lax.ppermute(block, axis, [(source, target)])


def place_kernel(widths, where_ref, *refs):
    mine, theirs, outs = refs[:5], refs[5:10], refs[10:-3]
    held, in_sems, out_sems = refs[-3:]
    section, core, side = (where_ref[i] for i in range(3))

    def run(same, other):
        steps = []
        for rank_core, pieces in ((core, mine), (1 - core, theirs)):
            entries = [(piece, i) for piece in pieces for i in range(piece.shape[0])]
            for i, (piece, entry) in enumerate(entries):
                block = (same, other, same, other)[i // 4]
                to_side = (side, side, 1 - side, 1 - side)[i // 4]
                slot = held.at[len(steps)]
                load = pltpu.make_async_copy(piece.at[entry], slot, in_sems.at[len(steps)])
                load.start()
                stores, start = [], 0
                for index, width in enumerate(widths):
                    target = outs[block * len(widths) + index].at[i % 4, rank_core * 2 + to_side]
                    stores.append((slot.at[:, start : start + width], target))
                    start += width
                steps.append((load, stores))
        begun = []
        for load, stores in steps:
            load.wait()
            for source, target in stores:
                store = pltpu.make_async_copy(source, target, out_sems.at[len(begun)])
                store.start()
                begun.append(store)
        for store in begun:
            store.wait()

    @pl.when(section == 0)
    def _():
        run(0, 1)

    @pl.when(section == 1)
    def _():
        run(1, 0)


def place(pieces, where, widths=None):
    rows, columns = pieces[0].shape[1:]
    kind = pieces[0].dtype
    widths = widths or (columns,)
    shapes = [jax.ShapeDtypeStruct((4, 4, rows, width), kind) for width in widths] * 2
    return pl.pallas_call(
        functools.partial(place_kernel, widths),
        out_shape=shapes,
        in_specs=[pl.BlockSpec(memory_space=pltpu.SMEM)]
        + [pl.BlockSpec(memory_space=pl.ANY)] * len(pieces),
        out_specs=[pl.BlockSpec(memory_space=pl.ANY)] * len(shapes),
        scratch_shapes=[
            pltpu.VMEM((32, rows, columns), kind),
            pltpu.SemaphoreType.DMA((32,)),
            pltpu.SemaphoreType.DMA((32 * len(widths),)),
        ],
        compiler_params=pltpu.CompilerParams(vmem_limit_bytes=14 * 1024 * 1024),
        cost_estimate=SHORT,
    )(where, *pieces)


def add_low(first, second):
    return (first.astype(jnp.float32) + second.astype(jnp.float32)).astype(jnp.bfloat16)


def pick(array, index, axis):
    return lax.dynamic_index_in_dim(array, index, axis, keepdims=False)


def local_call(kernel, where, arrays, outs, scratch=(), steps=1, kind=jnp.bfloat16, limit=16):
    def spec(shape, first):
        if first is None:
            return pl.BlockSpec(shape, lambda i: (0,) * len(shape))
        block = (1, *shape[1:])
        return pl.BlockSpec(block, lambda i: (first + i,) + (0,) * (len(shape) - 1))

    pairs = [item if isinstance(item, tuple) else (item, None) for item in arrays]
    return pl.pallas_call(
        kernel,
        grid=(steps,),
        out_shape=[jax.ShapeDtypeStruct(shape, kind) for shape in outs],
        in_specs=[pl.BlockSpec(memory_space=pltpu.SMEM)]
        + [spec(array.shape, first) for array, first in pairs],
        out_specs=[spec(shape, None if steps == 1 else 0) for shape in outs],
        scratch_shapes=list(scratch),
        compiler_params=pltpu.CompilerParams(vmem_limit_bytes=limit * 1024 * 1024),
        cost_estimate=SHORT,
    )(where, *(array for array, _ in pairs))


def across_kernel(where_ref, own, got, own_high, got_high, *outs):
    low_keep, low_send, high_keep, high_send = outs
    section, side = where_ref[0], where_ref[2]
    rows, half = low_keep.shape[2:]

    def total(first, second, to_side, start, width):
        place = (
            0,
            pl.ds(pl.multiple_of(to_side * rows, 16), rows),
            pl.ds(pl.multiple_of(start, 128), width),
        )
        return add_low(first[place], second[place])

    for to_side in range(2):
        low_keep[0, to_side] = total(own, got, to_side, section * half, half)
        low_send[0, to_side] = total(own, got, to_side, (1 - section) * half, half)
    high_keep[0] = total(own_high, got_high, side, 0, 2 * half)
    high_send[0] = total(own_high, got_high, 1 - side, 0, 2 * half)


def along_kernel(
    where_ref, low, high, low_got, high_got, low_keep, low_send, high_keep, high_send
):
    section, side = where_ref[0], where_ref[2]
    half = low_keep.shape[2]
    for to_side, target in ((side, low_keep), (1 - side, low_send)):
        target[0] = add_low(low[0, to_side], low_got[0, to_side])
    for to_section, target in ((section, high_keep), (1 - section, high_send)):
        columns = pl.ds(pl.multiple_of(to_section * half, 128), half)
        target[0] = add_low(high[0, :, columns], high_got[0, :, columns])


def shards_kernel(where_ref, low, high, low_got, high_got, own, *rest):
    sends, both = rest[:3], rest[3]
    here = where_ref[3]
    for shard in range(2):
        both[shard] = add_low(low[shard], low_got[shard])
        both[2 + shard] = add_low(high[shard], high_got[shard])
    own[...] = both[here]
    for i, target in enumerate(sends):
        target[...] = both[lax.rem(here + 3 - i, 4)]


def pairs_kernel(where_ref, low, high, low_got, high_got, keep, send):
    def put(own, other):
        own[...] = add_low(low[...], low_got[...])
        other[...] = add_low(high[...], high_got[...])

    @pl.when(where_ref[3] < 2)
    def _():
        put(keep, send)

    @pl.when(where_ref[3] >= 2)
    def _():
        put(send, keep)


def single_kernel(where_ref, own, got, keep, send):
    here = lax.rem(where_ref[3], 2)
    keep[...] = add_low(own[here], got[here])
    send[...] = add_low(own[1 - here], got[1 - here])


def back_kernel(counts, where_ref, *refs):
    keep, give = refs[-2:]

    def put(first, second):
        start = position = 0
        for pair in counts:
            width = refs[position].shape[1]
            for count, target in zip(pair, (first, second)):
                terms = refs[position : position + count]
                total = sum(term[...].astype(jnp.float32) for term in terms)
                target[:, start : start + width] = total.astype(jnp.bfloat16)
                position += count
            start += width

    @pl.when(where_ref[0] == 0)
    def _():
        put(keep, give)

    @pl.when(where_ref[0] == 1)
    def _():
        put(give, keep)


def grad_kernel(kinds, where_ref, *refs):
    count = len(kinds)
    lefts, rights = refs[:count], refs[count : 2 * count]
    own, send, sums, total = refs[2 * count :]
    core = where_ref[1]
    step = pl.program_id(0)

    def run(left, right):
        total[...] = contract_rows(left[...], right[...])
        sums[...] = jnp.sum(right[...].astype(jnp.float32), axis=0, keepdims=True)
        parts, rows = own.shape[:2]
        for part in range(parts):
            for to_core, target in ((core, own), (1 - core, send)):
                start = pl.multiple_of((2 * part + to_core) * rows, 32)
                target[part] = total[pl.ds(start, rows), :].astype(jnp.bfloat16)

    first = 0
    for kind, left, right in zip(kinds, lefts, rights):

        @pl.when((step >= first) & (step < first + kind))
        def _(left=left, right=right):
            run(left, right)

        first += kind


def grad_call(where, pairs, deep=False):
    width = 768
    row_count = pairs[0][0].shape[0]
    lefts, rights = [left for left, _ in pairs], [right for _, right in pairs]
    kinds = [max(left.shape[1], right.shape[1]) // width for left, right in pairs]
    steps = sum(kinds)
    firsts = [sum(kinds[:index]) for index in range(len(kinds))]

    def spec(wide, first, kind):
        if not wide:
            return pl.BlockSpec((row_count, width), lambda j: (0, 0))
        return pl.BlockSpec((row_count, width), lambda j: (0, jnp.clip(j - first, 0, kind - 1)))

    in_specs = [pl.BlockSpec(memory_space=pltpu.SMEM)]
    for arrays in (lefts, rights):
        for array, first, kind in zip(arrays, firsts, kinds):
            in_specs.append(spec(array.shape[1] > width, first, kind))
    if deep:
        shape, block = (4, lefts[0].shape[1] // 8, width), (1, lefts[0].shape[1] // 8, width)
        out_spec = pl.BlockSpec(block, lambda j: (j, 0, 0))
        sums_shape, sums_spec = (1, width), pl.BlockSpec((1, width), lambda j: (0, 0))
    else:
        shape, block = (4, width // 8, steps * width), (4, width // 8, width)
        out_spec = pl.BlockSpec(block, lambda j: (0, 0, j))
        sums_shape, sums_spec = (1, steps * width), pl.BlockSpec((1, width), lambda j: (0, j))
    return pl.pallas_call(
        functools.partial(grad_kernel, kinds),
        grid=(steps,),
        out_shape=[jax.ShapeDtypeStruct(shape, jnp.bfloat16)] * 2
        + [jax.ShapeDtypeStruct(sums_shape, jnp.float32)],
        in_specs=in_specs,
        out_specs=[out_spec, out_spec, sums_spec],
        scratch_shapes=[pltpu.VMEM((width, width), jnp.float32)],
        compiler_params=pltpu.CompilerParams(vmem_limit_bytes=16 * 1024 * 1024),
        cost_estimate=SHORT,
    )(where, *lefts, *rights)


GELU_SCALE = 0.7978845608028654
GELU_CUBE = 0.044715


def expand_kernel(normed_ref, weight_ref, bias_ref, active_ref, slope_ref):
    values = jnp.dot(normed_ref[...], weight_ref[...], preferred_element_type=jnp.float32)
    values = values + bias_ref[...]
    square = values * values
    bent = jnp.tanh(GELU_SCALE * values * (1.0 + GELU_CUBE * square))
    half = 0.5 * (1.0 + bent)
    active_ref[...] = (values * half).astype(jnp.bfloat16)
    inner = GELU_SCALE * (1.0 + 3.0 * GELU_CUBE * square)
    slope_ref[...] = (half + 0.5 * values * (1.0 - bent * bent) * inner).astype(jnp.bfloat16)


def expand_call(normed, weight, bias):
    row_count, depth = normed.shape
    columns = weight.shape[1]
    width = depth
    out_spec = pl.BlockSpec((row_count, width), lambda j: (0, j))
    return pl.pallas_call(
        expand_kernel,
        grid=(columns // width,),
        out_shape=[jax.ShapeDtypeStruct((row_count, columns), jnp.bfloat16)] * 2,
        in_specs=[
            pl.BlockSpec((row_count, depth), lambda j: (0, 0)),
            pl.BlockSpec((depth, width), lambda j: (0, j)),
            pl.BlockSpec((1, width), lambda j: (0, j)),
        ],
        out_specs=[out_spec, out_spec],
        compiler_params=pltpu.CompilerParams(vmem_limit_bytes=24 * 1024 * 1024),
        cost_estimate=SHORT,
    )(normed, weight, bias[None])


def ordered(own, other, index, axis):
    first = jnp.where(index == 0, own, other)
    second = jnp.where(index == 0, other, own)
    return jnp.concatenate([first, second], axis=axis)


class Moves:
    def __init__(self, where):
        self.where = where

    over_x = staticmethod(lambda array: swap(array, "section", 1))
    over_y = staticmethod(lambda array: swap(array, "replica", 2))
    to_mate = staticmethod(lambda array: swap(array, "replica", 1))

    def gather(self):
        def along(own):
            return ((), [(own, lambda array: lax.all_gather(array, "shard", axis=0))])

        along.late = 1

        def across(chunks):
            return ((chunks,), [(chunks, self.over_x), (chunks, self.over_y)])

        def beyond(*arrays):
            _, over_x, over_y = arrays
            return (arrays, [(over_x[:2], self.over_y), (over_y[2:], self.over_x)])

        return [along, across, beyond]

    def laid(self, state, widths=None):
        theirs = tuple(self.to_mate(piece) for piece in state)
        return place((*state, *theirs), self.where, widths)

    def reduce(self, direct):
        def mates(own, send):
            return ((own,), [(send, self.to_mate)])

        def across(own, got):
            shards, rows, columns = own.shape
            low = (2, 2, rows // 2, columns // 2)
            high = (2, rows // 2, columns)
            result = local_call(
                across_kernel,
                self.where,
                ((own, 0), (got, 0), (own, 2), (got, 2)),
                (low, low, high, high),
                steps=2,
            )
            low_keep, low_send, high_keep, high_send = result
            return ((low_keep, high_keep), [(low_send, self.over_x), (high_send, self.over_y)])

        def along(*state):
            shape = (2, *state[0].shape[2:])
            result = local_call(
                along_kernel, self.where, [(array, 0) for array in state], (shape,) * 4, steps=2
            )
            low_keep, low_send, high_keep, high_send = result
            return ((low_keep, high_keep), [(low_send, self.over_y), (high_send, self.over_x)])

        def shards(*state):
            shape = state[0].shape[1:]
            scratch = [pltpu.VMEM((4, *shape), jnp.bfloat16)]
            result = local_call(shards_kernel, self.where, state, (shape,) * 4, scratch)
            turns = [functools.partial(turn, axis="shard", step=i) for i in (1, 2, 3)]
            return ((result[0],), list(zip(result[1:], turns)))

        def pairs(*state):
            shape = state[0].shape
            keep, send = local_call(pairs_kernel, self.where, state, (shape, shape))
            return ((keep,), [(send, lambda array: swap(array, "shard", 2))])

        def single(own, got):
            shape = own.shape[1:]
            keep, send = local_call(single_kernel, self.where, (own, got), (shape, shape))
            return ((keep,), [(send, lambda array: swap(array, "shard", 1))])

        return [mates, across, along] + ([shards] if direct else [pairs, single])

    def spread(self):
        def back(*pairs):
            terms = [term for pair in pairs for state in pair for term in state]
            rows = terms[0].shape[0]
            shape = (rows, sum(pair[0][0].shape[1] for pair in pairs))
            counts = [tuple(len(state) for state in pair) for pair in pairs]
            kernel = functools.partial(back_kernel, counts)
            keep, give = local_call(kernel, self.where, terms, (shape, shape))
            return ((keep,), [(give, self.over_x)])

        def around(keep, got):
            rows = jnp.stack([keep, got])

            def corner(array):
                over_y = self.over_y(array)
                return (over_y, self.to_mate(over_y))

            return ((rows,), [(rows, self.to_mate), (rows, corner)])

        return [back, around]

    @staticmethod
    def exchange(late):
        def step(section, first, second):
            give = jnp.where(section == 0, second, first)
            if not late:
                return ((), [(give, Moves.over_x)])
            return ((), [(give, lambda array: lax.all_gather(array, "section", axis=0))])

        step.late = late
        return [step]

    def total(self):
        def chip(array):
            return ((array,), [(array, self.to_mate)])

        def step_of(move):
            def step(own, got):
                array = own + got
                return ((array,), [(array, move)])

            return step

        moves = (self.over_x, self.over_y, lambda a: swap(a, "shard", 2), lambda a: swap(a, "shard", 1))
        return [chip] + [step_of(move) for move in moves]


class Flows:
    def __init__(self):
        self.left = {}
        self.states = {}
        self.open = {}

    def start(self, name, steps, *state):
        self.left[name] = list(steps)
        self.states[name] = state

    def extend(self, name, steps):
        self.left[name] += steps

    def stage(self, compute=lambda: (), *inputs):
        names = [name for name in self.left if self.left[name]]
        steps = {name: self.left[name].pop(0) for name in names}
        names = [name for name in names if steps[name] is not None]
        steps = [steps[name] for name in names]
        states = [self.states[name] for name in names]
        inputs, states = lax.optimization_barrier((inputs, states))
        ready = [step(*state) for step, state in zip(steps, states)]
        kept = [keep for keep, _ in ready]
        sent = [[array for array, _ in sends] for _, sends in ready]
        inputs, kept, sent = lax.optimization_barrier((inputs, kept, sent))
        got = [
            [move(array) for array, (_, move) in zip(arrays, sends)]
            for arrays, (_, sends) in zip(sent, ready)
        ]
        late = [getattr(step, "late", 0) for step in steps]
        waited = [result for result, slow in zip(got, late) if not slow]
        due = [name for name in self.open if self.open[name] == 1]
        closing = [self.states[name] for name in due]
        results, waited, closing = lax.optimization_barrier((compute(*inputs), waited, closing))
        self.states.update(zip(due, closing))
        self.open = {name: left - 1 for name, left in self.open.items() if left > 1}
        self.open.update({name: slow for name, slow in zip(names, late) if slow})
        waited = iter(waited)
        for name, keep, result, slow in zip(names, kept, got, late):
            self.states[name] = (*keep, *(result if slow else next(waited)))
        return results


def close_kernel(where_ref, *refs):
    section, core, side = (where_ref[i] for i in range(3))
    wide_pieces, last_pieces = refs[:4], refs[4:8]
    input_out, expand_out, output_out, contract_out = refs[8:]
    input_half = input_out.shape[1] // 2
    contract_half = contract_out.shape[1] // 2
    split = expand_out.shape[1] - (wide_pieces[0].shape[2] - input_half)

    def one(far_core, far_side, far_section):
        at_section = section if far_section == 0 else 1 - section
        at_side = side if far_side == 0 else 1 - side
        at_core = core if far_core == 0 else 1 - core
        rank = at_core * 2 + at_side
        wide = wide_pieces[far_core * 2 + far_side][far_section].astype(jnp.float32)
        rows = pl.ds(pl.multiple_of(rank * wide.shape[0], 16), wide.shape[0])
        columns = pl.ds(pl.multiple_of(at_section * input_half, 128), input_half)
        input_out[rows, columns] = wide[:, :input_half]
        wide = wide[:, input_half:]

        @pl.when(at_section == 0)
        def _():
            expand_out[rows, : wide.shape[1]] = wide

        @pl.when(at_section == 1)
        def _():
            expand_out[rows, wide.shape[1] :] = wide[:, :split]
            output_out[rows, :] = wide[:, split:]

        last = last_pieces[far_core * 2 + far_side][far_section].astype(jnp.float32)
        rows = pl.ds(pl.multiple_of(rank * last.shape[0], 16), last.shape[0])
        columns = pl.ds(pl.multiple_of(at_section * contract_half, 128), contract_half)
        contract_out[rows, columns] = last

    for far_core in range(2):
        for far_side in range(2):
            for far_section in range(2):
                one(far_core, far_side, far_section)


def close(where, wide, contract, shapes):
    def pieces(state):
        own, mate, (over_y, mate_y) = state
        return (own, over_y, mate, mate_y)

    arrays = (*pieces(wide), *pieces(contract))
    return local_call(close_kernel, where, arrays, shapes, kind=jnp.float32, limit=32)

VECTORS = ("gain_a", "shift_a", "bias_q", "bias_v", "bias_o", "gain_f", "shift_f", "bias_c")


def forward_attention(params, hidden_low, segment):
    hidden = hidden_low.astype(jnp.float32)
    normed, stats_a = layer_norm(hidden, params["gain_a"], params["shift_a"])
    normed = normed.astype(jnp.bfloat16)
    zeros = jnp.zeros_like(params["bias_q"])
    joint_bias = jnp.concatenate([params["bias_q"], zeros, params["bias_v"]])
    joint_low = (
        jnp.dot(normed, params["input"], preferred_element_type=jnp.float32) + joint_bias
    ).astype(jnp.bfloat16)
    mixed_low, log_sums = attend_forward(joint_low, segment)
    middle = (
        hidden
        + jnp.dot(mixed_low, params["output"], preferred_element_type=jnp.float32)
        + params["bias_o"]
    )
    return dict(
        hidden_low=hidden_low,
        normed=normed,
        stats_a=stats_a,
        joint_low=joint_low,
        log_sums=log_sums,
        mixed_low=mixed_low,
        middle=middle,
    )


def forward_expand(params, middle):
    normed_two, stats_f = layer_norm(middle, params["gain_f"], params["shift_f"])
    normed_two = normed_two.astype(jnp.bfloat16)
    activated, slope = expand_call(normed_two, params["expand"], params["bias_e"])
    return dict(normed_two=normed_two, stats_f=stats_f, slope=slope, activated=activated)


def forward_contract(params, middle, activated, living):
    result = (
        middle
        + jnp.dot(activated, params["contract"], preferred_element_type=jnp.float32)
        + params["bias_c"]
    )
    return (result * living[:, None]).astype(jnp.bfloat16)


class Backward:
    def __init__(self, params, kept, segment, living, where, upstream):
        self.params, self.segment, self.living, self.where = params, segment, living, where
        self.held = dict(kept, upstream=upstream)

    def run(self, flow, part):
        function, names = {
            "expand": (self.expand, ("upstream", "activated", "slope")),
            "norm": (
                self.norm,
                ("expand_low", "normed_two", "out_grad", "middle", "stats_f", "mixed_low"),
            ),
            "attention": (self.attention, ("joint_low", "log_sums", "mixed_grad")),
            "input": (self.input, ("normed", "joint_grad")),
            "last": (self.last, ("joint_grad", "middle_grad", "hidden_low", "stats_a")),
            "both": (
                self.both,
                ("normed", "joint_grad", "middle_grad", "hidden_low", "stats_a"),
            ),
        }[part]
        self.held.update(flow.stage(function, *(self.held[name] for name in names)))

    def grads(self, name, *pairs, deep=False):
        if self.where is not None:
            own, send, sums = grad_call(self.where, pairs, deep)
            return {name + "_own": own, name + "_send": send, name + "_sums": sums[0]}
        whole = jnp.concatenate([contract_rows(*pair).astype(jnp.bfloat16) for pair in pairs], axis=1)
        sums = [jnp.sum(right.astype(jnp.float32), axis=0) for _, right in pairs]
        return {name + "_own": whole, name + "_sums": jnp.concatenate(sums)}

    def expand(self, upstream, activated, slope):
        out_grad = upstream.astype(jnp.float32) * self.living[:, None]
        low = out_grad.astype(jnp.bfloat16)
        found = self.grads("contract", (activated, low), deep=True)
        activated_grad = times_transpose(low, self.params["contract"])
        expand_low = (activated_grad * slope.astype(jnp.float32)).astype(jnp.bfloat16)
        return dict(found, out_grad=out_grad, expand_low=expand_low)

    def norm(self, expand_low, normed_two, out_grad, middle, stats_f, mixed_low):
        normed_grad = times_transpose(expand_low, self.params["expand"])
        norm_grad, gain_grad, shift_grad = layer_norm_back(
            middle, stats_f, self.params["gain_f"], normed_grad
        )
        middle_grad = out_grad + norm_grad
        branch_low = middle_grad.astype(jnp.bfloat16)
        mixed_grad = times_transpose(branch_low, self.params["output"]).astype(jnp.bfloat16)
        found = self.grads("expand", (normed_two, expand_low), (mixed_low, branch_low))
        return dict(
            found, middle_grad=middle_grad, mixed_grad=mixed_grad, gain_f=gain_grad, shift_f=shift_grad
        )

    def attention(self, joint_low, log_sums, mixed_grad):
        return dict(joint_grad=attend_backward(joint_low, log_sums, mixed_grad, self.segment))

    def input(self, normed, joint_grad):
        return self.grads("input", (normed, joint_grad))

    def last(self, joint_grad, middle_grad, hidden_low, stats_a):
        normed_grad = times_transpose(joint_grad, self.params["input"])
        norm_grad, gain_grad, shift_grad = layer_norm_back(
            hidden_low.astype(jnp.float32), stats_a, self.params["gain_a"], normed_grad
        )
        grad = middle_grad + norm_grad
        return dict(grad_low=grad.astype(jnp.bfloat16), gain_a=gain_grad, shift_a=shift_grad)

    def both(self, normed, joint_grad, middle_grad, hidden_low, stats_a):
        found = self.input(normed, joint_grad)
        return dict(found, **self.last(joint_grad, middle_grad, hidden_low, stats_a))

    def small(self):
        held = self.held
        width = held["gain_a"].shape[0]
        split = held["expand_sums"].shape[0] - width
        held = dict(
            held,
            bias_q=held["input_sums"][:width],
            bias_v=held["input_sums"][2 * width :],
            bias_o=held["expand_sums"][split:],
            bias_c=held["contract_sums"],
        )
        vectors = [held[name] for name in VECTORS] + [held["expand_sums"][:split]]
        return jnp.concatenate(vectors).reshape(-1, width)


def per_device(
    tokens,
    cotangent,
    lengths,
    assignment,
    attention_gain,
    attention_shift,
    input_weight,
    query_bias,
    value_bias,
    output_weight,
    output_bias,
    feedforward_gain,
    feedforward_shift,
    expand_weight,
    expand_bias,
    contract_weight,
    contract_bias,
):
    section = lax.axis_index("section")
    shard = lax.axis_index("shard")
    replica = lax.axis_index("replica")
    shards, replicas = lax.axis_size("shard"), lax.axis_size("replica")
    core, side = replica % 2, replica // 2
    model_width = tokens.shape[1]
    cube = shards == 4 and replicas == 4
    where = jnp.stack([section, core, side, shard]).astype(jnp.int32)

    slot = (shard * replicas + replica) * MICRO + section
    matches = (assignment == slot).astype(jnp.int32)
    counts = jnp.sum(matches[:, None] * lengths, axis=0, dtype=jnp.int32)
    segment, living = slot_layout(counts, ROWS)
    entering = lax.dynamic_slice_in_dim(tokens, section * ROWS, ROWS, 0)
    seed = lax.dynamic_slice_in_dim(cotangent, section * ROWS, ROWS, 0)

    vectors = (
        attention_gain,
        attention_shift,
        query_bias,
        value_bias,
        output_bias,
        feedforward_gain,
        feedforward_shift,
        contract_bias,
        expand_bias,
    )
    small_own = jnp.concatenate(vectors, axis=1)
    expand_width = expand_weight.shape[2]
    flow = Flows()
    moves = Moves(where)

    def joined(members):
        return [member.reshape(-1, member.shape[-1]) for member in members]

    def named(small_all, **pairs):
        count = len(VECTORS)
        split = small_all.shape[2] - expand_bias.shape[1]
        lines = small_all[:, :, :split].reshape(2, shards, count, split // count)
        lines = lines.transpose(0, 2, 1, 3).reshape(2, count, model_width).astype(jnp.float32)
        bias_e = small_all[:, :, split:].reshape(2, expand_width).astype(jnp.float32)
        found = []
        for block in range(2):
            params = {name: lines[block, index] for index, name in enumerate(VECTORS)}
            params["bias_e"] = bias_e[block]
            params.update({name: pair[block] for name, pair in pairs.items()})
            found.append(params)
        return found

    if cube:

        def chunk(weight):
            size = weight.shape[1] // 4
            return lax.dynamic_slice_in_dim(weight[0], (core * 2 + side) * size, size, 0)

        input_chunk, output_chunk = chunk(input_weight), chunk(output_weight)
        small_rows = small_own.shape[1] // 128
        short = input_chunk.shape[0] - small_rows
        padded = jnp.pad(small_own.reshape(small_rows, 128), ((0, short), (0, 0)))
        opening = jnp.concatenate([input_chunk, output_chunk, padded], axis=1)
        widths = (input_chunk.shape[1], output_chunk.shape[1], 128)
        flow.start("gather_open", moves.gather(), opening)
        flow.stage()
        flow.start("gather_expand", moves.gather(), chunk(expand_weight))
        flow.stage()
        flow.start("gather_contract", moves.gather(), chunk(contract_weight))
        flow.stage()

        def open_part(state, hidden_low):
            laid = moves.laid(state, widths)
            small_all = jnp.stack(laid[2::3])[:, :, 0, :small_rows].reshape(2, shards, -1)
            found = named(small_all, input=joined(laid[0::3]), output=joined(laid[1::3]))
            return (found, forward_attention(found[0], hidden_low, segment))

        (params, kept_first) = flow.stage(open_part, flow.states["gather_open"], entering)

        def middle_part(state, middle):
            expand_all = joined(moves.laid(state))
            held = forward_expand(dict(params[0], expand=expand_all[0]), middle)
            return (expand_all, held)

        expand_all, held = flow.stage(
            middle_part, flow.states["gather_expand"], kept_first["middle"]
        )
        kept_first.update(held)
        contract_all = joined(moves.laid(flow.states["gather_contract"]))
        for block in range(2):
            params[block].update(expand=expand_all[block], contract=contract_all[block])
    else:

        def whole(weight):
            held = lax.all_gather(weight, "shard", axis=1, tiled=True)
            return lax.all_gather(held, "section", axis=0, tiled=True)

        params = named(
            whole(small_own[None]),
            input=whole(input_weight),
            output=whole(output_weight),
            expand=whole(expand_weight),
            contract=whole(contract_weight),
        )
        kept_first = forward_attention(params[0], entering, segment)
        kept_first.update(forward_expand(params[0], kept_first["middle"]))

    middle_out = forward_contract(
        params[0], kept_first["middle"], kept_first["activated"], living
    )

    def second_forward(hidden_low):
        kept = forward_attention(params[1], hidden_low, segment)
        kept.update(forward_expand(params[1], kept["middle"]))
        return (kept, forward_contract(params[1], kept["middle"], kept["activated"], living))

    kept_second, last_out = second_forward(middle_out)

    def begin(block, name, direct=False):
        tag = ("first_" if block is first else "second_") + name
        if cube:
            flow.start(tag, moves.reduce(direct), block.held[name + "_own"], block.held[name + "_send"])

    def spread(name, *members):
        if cube:
            pairs = [(flow.states["first_" + m], flow.states["second_" + m]) for m in members]
            back, around = moves.spread()
            steps = [back, around] if name == "wide" else [back, None, around]
            flow.start(name, steps, *pairs)

    first = None
    second = Backward(params[1], kept_second, segment, living, where if cube else None, seed)
    flow.start("out", moves.exchange(0), section, middle_out, last_out)
    second.run(flow, "expand")
    begin(second, "contract")
    second.run(flow, "norm")
    begin(second, "expand")
    second.run(flow, "attention")
    second.run(flow, "both")
    begin(second, "input")

    first = Backward(params[0], kept_first, segment, living, where if cube else None, second.held["grad_low"])
    first.run(flow, "expand")
    begin(first, "contract")
    first.run(flow, "norm")
    begin(first, "expand")
    first.run(flow, "attention")
    first.run(flow, "input")
    begin(first, "input", direct=True)
    first.run(flow, "last")
    small_both = jnp.stack([first.small(), second.small()])
    flow.start("small", moves.total() if cube else [], small_both)
    flow.start("grad", moves.exchange(4), section, first.held["grad_low"], second.held["grad_low"])
    flow.stage()
    spread("contract", "contract")
    flow.stage()
    flow.stage()
    spread("wide", "input", "expand")
    flow.stage()
    flow.stage()

    def own_block(name, first_value, second_value):
        keep = jnp.where(section == 0, first_value, second_value)
        got = flow.states[name][0]
        got = pick(got, 1 - section, 0) if got.ndim == 3 else got
        return ordered(keep, got, section, 0)

    block_out = own_block("out", middle_out, last_out)
    grad_out = own_block("grad", first.held["grad_low"], second.held["grad_low"])
    grad_out = grad_out.astype(jnp.float32)

    if cube:
        small_sum = flow.states["small"][0] + flow.states["small"][1]
        shapes = [
            weight.shape[1:] for weight in (input_weight, expand_weight, output_weight, contract_weight)
        ]
        large = close(where, flow.states["wide"], flow.states["contract"], shapes)
    else:
        small_sum = lax.psum(small_both, ("section", "shard", "replica"))
        large = []
        for name in ("input_own", "expand_own", "contract_own"):
            wide = jnp.stack([block.held[name] for block in (first, second)])
            held = lax.psum_scatter(wide, "section", scatter_dimension=0, tiled=True)
            held = lax.psum_scatter(held[0], "shard", scatter_dimension=0, tiled=True)
            large.append(lax.psum(held, "replica").astype(jnp.float32))
        large[1:2] = [large[1][:, :expand_width], large[1][:, expand_width:]]
    small_sum = pick(small_sum, section, 0)
    lines = small_sum[: len(VECTORS)].reshape(len(VECTORS), shards, -1)
    lines = pick(lines, shard, 1)
    small = {name: lines[index][None] for index, name in enumerate(VECTORS)}
    bias_e_grad = pick(small_sum[len(VECTORS) :].reshape(shards, -1), shard, 0)[None]
    input_grad, expand_grad, output_grad, contract_grad = (member[None] for member in large)
    return (
        block_out[None],
        grad_out[None],
        small["gain_a"],
        small["shift_a"],
        input_grad,
        small["bias_q"],
        small["bias_v"],
        output_grad,
        small["bias_o"],
        small["gain_f"],
        small["shift_f"],
        expand_grad,
        bias_e_grad,
        contract_grad,
        small["bias_c"],
    )


def solution(mesh):
    placed = (
        P(("shard", "replica"), None),
        P(("shard", "replica"), None),
        P(),
        P(),
        P("section", "shard"),
        P("section", "shard"),
        P("section", "shard", None),
        P("section", "shard"),
        P("section", "shard"),
        P("section", "shard", None),
        P("section", "shard"),
        P("section", "shard"),
        P("section", "shard"),
        P("section", "shard", None),
        P("section", "shard"),
        P("section", "shard", None),
        P("section", "shard"),
    )
    return jax.shard_map(
        per_device,
        mesh=mesh,
        in_specs=placed,
        out_specs=(
            P("section", ("shard", "replica"), None),
            P("section", ("shard", "replica"), None),
            P("section", "shard"),
            P("section", "shard"),
            P("section", "shard", None),
            P("section", "shard"),
            P("section", "shard"),
            P("section", "shard", None),
            P("section", "shard"),
            P("section", "shard"),
            P("section", "shard"),
            P("section", "shard", None),
            P("section", "shard"),
            P("section", "shard", None),
            P("section", "shard"),
        ),
        check_vma=False,
    )
```

```python
import functools

import jax
import jax.numpy as jnp
from jax import lax
from jax.experimental import pallas as pl
from jax.experimental.pallas import tpu as pltpu
from jax.sharding import PartitionSpec as P

HEADS = 12
ROWS = 512
MICRO = 2


EPSILON = 1e-05
MASKED_SCORE = -1e30

SHORT = pl.CostEstimate(flops=1, bytes_accessed=1, transcendentals=0)


def layer_norm(hidden, norm_gain, norm_shift):
    mean = jnp.mean(hidden, axis=-1, keepdims=True)
    center = hidden - mean
    spread = jnp.mean(center * center, axis=-1, keepdims=True)
    scale = lax.rsqrt(spread + EPSILON)
    return (center * scale * norm_gain + norm_shift, (mean, scale))


def layer_norm_back(hidden, stats, norm_gain, grad):
    mean, scale = stats
    hat = (hidden - mean) * scale
    scaled = grad * norm_gain
    first = jnp.mean(scaled, axis=-1, keepdims=True)
    second = jnp.mean(scaled * hat, axis=-1, keepdims=True)
    hidden_grad = scale * (scaled - first - hat * second)
    return (hidden_grad, jnp.sum(grad * hat, axis=0), jnp.sum(grad, axis=0))


def slot_layout(counts, row_count):
    bounds = jnp.cumsum(counts, dtype=jnp.int32)
    places = jnp.arange(row_count, dtype=jnp.int32)
    segment = jnp.sum(
        (bounds[None, :] <= places[:, None]).astype(jnp.int32), axis=1, dtype=jnp.int32
    )
    living = (places < bounds[-1]).astype(jnp.float32)
    return (segment, living)


def gelu_tanh(values):
    return jax.nn.gelu(values, approximate=True)


def contract_rows(left_side, right_side):
    return lax.dot_general(
        left_side, right_side, (((0,), (0,)), ((), ())), preferred_element_type=jnp.float32
    )


def times_transpose(left_side, right_side):
    return lax.dot_general(
        left_side, right_side, (((1,), (1,)), ((), ())), preferred_element_type=jnp.float32
    )


def masked_bias(segment_column, segment_row):
    row_count = segment_column.shape[0]
    query_places = lax.broadcasted_iota(jnp.int32, (row_count, row_count), 0)
    key_places = lax.broadcasted_iota(jnp.int32, (row_count, row_count), 1)
    allowed = (segment_column == segment_row) & (key_places <= query_places)
    return jnp.where(allowed, 0.0, MASKED_SCORE)


def head_lanes(block, head):
    half = block.shape[1] // 2
    lanes = lax.broadcasted_iota(jnp.int32, block.shape, 1)
    return jnp.where((lanes < half) == (head == 0), block, jnp.zeros_like(block))


def attend_kernel(column_ref, row_ref, q_ref, k_ref, v_ref, mixed_ref, log_ref, bias_ref):
    @pl.when(pl.program_id(0) == 0)
    def _():
        bias_ref[...] = masked_bias(column_ref[...], row_ref[...])

    row_count, width = q_ref.shape
    tall = row_count // 2
    scale = (width // 2) ** (-0.5)
    first_lanes = lax.broadcasted_iota(jnp.int32, (tall, width), 1) < width // 2
    for start in (0, tall):
        stop = start + tall
        queries = q_ref[start:stop] * jnp.asarray(scale, q_ref.dtype)
        outs, logs = [], []
        for head in range(2):
            scores = times_transpose(head_lanes(queries, head), k_ref[:stop])
            scores = scores + bias_ref[start:stop, :stop]
            row_max = jnp.max(scores, axis=1, keepdims=True)
            exponent = jnp.exp(scores - row_max)
            row_total = jnp.sum(exponent, axis=1, keepdims=True)
            probs = (exponent * (1.0 / row_total)).astype(jnp.bfloat16)
            outs.append(jnp.dot(probs, v_ref[:stop], preferred_element_type=jnp.float32))
            logs.append(jnp.broadcast_to(row_max + jnp.log(row_total), (tall, width)))
        mixed_ref[start:stop] = jnp.where(first_lanes, *outs).astype(jnp.bfloat16)
        log_ref[start:stop] = jnp.where(first_lanes, *logs)


def attend_back_kernel(
    column_ref, row_ref, q_ref, k_ref, v_ref, grad_ref, log_ref, dq_ref, dk_ref, dv_ref, bias_ref
):
    @pl.when(pl.program_id(0) == 0)
    def _():
        bias_ref[...] = masked_bias(column_ref[...], row_ref[...])

    row_count, width = q_ref.shape
    tall = row_count // 2
    scale = (width // 2) ** (-0.5)
    first_lanes = lax.broadcasted_iota(jnp.int32, (tall, width), 1) < width // 2
    key_parts, value_parts = [], []
    for start in (0, tall):
        stop = start + tall
        queries = q_ref[start:stop] * jnp.asarray(scale, q_ref.dtype)
        query_parts = []
        key_grad = value_grad = 0.0
        for head in range(2):
            mine = head_lanes(queries, head)
            grad = head_lanes(grad_ref[start:stop], head)
            lane = head * (width // 2)
            scores = times_transpose(mine, k_ref[:stop]) + bias_ref[start:stop, :stop]
            probs = jnp.exp(scores - log_ref[start:stop, lane : lane + 1])
            prob_grad = times_transpose(grad, v_ref[:stop])
            center = jnp.sum(prob_grad * probs, axis=1, keepdims=True)
            score_grad = (probs * (prob_grad - center)).astype(jnp.bfloat16)
            query_parts.append(
                jnp.dot(score_grad, k_ref[:stop], preferred_element_type=jnp.float32)
            )
            key_grad = key_grad + contract_rows(score_grad, mine)
            value_grad = value_grad + contract_rows(probs.astype(jnp.bfloat16), grad)
        dq_ref[start:stop] = (jnp.where(first_lanes, *query_parts) * scale).astype(jnp.bfloat16)
        key_parts.append(key_grad)
        value_parts.append(value_grad)
    for parts, target in ((key_parts, dk_ref), (value_parts, dv_ref)):
        target[:tall] = (parts[0] + parts[1][:tall]).astype(jnp.bfloat16)
        target[tall:] = parts[1][tall:].astype(jnp.bfloat16)


def attention_call(kernel, segment, blocks, outs):
    row_count = segment.shape[0]
    pairs = HEADS // 2
    model_width = blocks[0][0].shape[1] // 3
    lanes = model_width // pairs

    def spec(first):
        return pl.BlockSpec((row_count, lanes), lambda pair: (0, first + pair))

    return pl.pallas_call(
        kernel,
        grid=(pairs,),
        out_shape=[jax.ShapeDtypeStruct((row_count, model_width), kind) for kind in outs],
        in_specs=[
            pl.BlockSpec((row_count, 1), lambda pair: (0, 0)),
            pl.BlockSpec((1, row_count), lambda pair: (0, 0)),
        ]
        + [spec(first) for _, first in blocks],
        out_specs=[spec(0) for _ in outs],
        scratch_shapes=[pltpu.VMEM((row_count, row_count), jnp.float32)],
        compiler_params=pltpu.CompilerParams(vmem_limit_bytes=20 * 1024 * 1024),
        cost_estimate=SHORT,
    )(segment[:, None], segment[None, :], *(array for array, _ in blocks))


def attend_forward(joint_low, segment):
    pairs = HEADS // 2
    blocks = [(joint_low, first * pairs) for first in range(3)]
    return attention_call(attend_kernel, segment, blocks, (jnp.bfloat16, jnp.float32))


def attend_backward(joint_low, log_sums, mixed_grad, segment):
    pairs = HEADS // 2
    blocks = [(joint_low, first * pairs) for first in range(3)]
    blocks += [(mixed_grad, 0), (log_sums, 0)]
    parts = attention_call(attend_back_kernel, segment, blocks, (jnp.bfloat16,) * 3)
    return jnp.concatenate(parts, axis=1)


def swap(block, axis, bit):
    return lax.ppermute(block, axis, [(i, i ^ bit) for i in range(lax.axis_size(axis))])


def turn(block, axis, step):
    size = lax.axis_size(axis)
    return lax.ppermute(block, axis, [((i + step) % size, i) for i in range(size)])


def one_way(block, axis, source, target):
    return lax.ppermute(block, axis, [(source, target)])


def place_kernel(widths, where_ref, *refs):
    mine, theirs, outs = refs[:5], refs[5:10], refs[10:-3]
    held, in_sems, out_sems = refs[-3:]
    section, core, side = (where_ref[i] for i in range(3))

    def run(same, other):
        steps = []
        for rank_core, pieces in ((core, mine), (1 - core, theirs)):
            entries = [(piece, i) for piece in pieces for i in range(piece.shape[0])]
            for i, (piece, entry) in enumerate(entries):
                block = (same, other, same, other)[i // 4]
                to_side = (side, side, 1 - side, 1 - side)[i // 4]
                slot = held.at[len(steps)]
                load = pltpu.make_async_copy(piece.at[entry], slot, in_sems.at[len(steps)])
                load.start()
                stores, start = [], 0
                for index, width in enumerate(widths):
                    target = outs[block * len(widths) + index].at[i % 4, rank_core * 2 + to_side]
                    stores.append((slot.at[:, start : start + width], target))
                    start += width
                steps.append((load, stores))
        begun = []
        for load, stores in steps:
            load.wait()
            for source, target in stores:
                store = pltpu.make_async_copy(source, target, out_sems.at[len(begun)])
                store.start()
                begun.append(store)
        for store in begun:
            store.wait()

    @pl.when(section == 0)
    def _():
        run(0, 1)

    @pl.when(section == 1)
    def _():
        run(1, 0)


def place(pieces, where, widths=None):
    rows, columns = pieces[0].shape[1:]
    kind = pieces[0].dtype
    widths = widths or (columns,)
    shapes = [jax.ShapeDtypeStruct((4, 4, rows, width), kind) for width in widths] * 2
    return pl.pallas_call(
        functools.partial(place_kernel, widths),
        out_shape=shapes,
        in_specs=[pl.BlockSpec(memory_space=pltpu.SMEM)]
        + [pl.BlockSpec(memory_space=pl.ANY)] * len(pieces),
        out_specs=[pl.BlockSpec(memory_space=pl.ANY)] * len(shapes),
        scratch_shapes=[
            pltpu.VMEM((32, rows, columns), kind),
            pltpu.SemaphoreType.DMA((32,)),
            pltpu.SemaphoreType.DMA((32 * len(widths),)),
        ],
        compiler_params=pltpu.CompilerParams(vmem_limit_bytes=14 * 1024 * 1024),
        cost_estimate=SHORT,
    )(where, *pieces)


def add_low(first, second):
    return (first.astype(jnp.float32) + second.astype(jnp.float32)).astype(jnp.bfloat16)


def pick(array, index, axis):
    return lax.dynamic_index_in_dim(array, index, axis, keepdims=False)


def local_call(kernel, where, arrays, outs, scratch=(), steps=1, kind=jnp.bfloat16, limit=16):
    def spec(shape, first):
        if first is None:
            return pl.BlockSpec(shape, lambda i: (0,) * len(shape))
        block = (1, *shape[1:])
        return pl.BlockSpec(block, lambda i: (first + i,) + (0,) * (len(shape) - 1))

    pairs = [item if isinstance(item, tuple) else (item, None) for item in arrays]
    return pl.pallas_call(
        kernel,
        grid=(steps,),
        out_shape=[jax.ShapeDtypeStruct(shape, kind) for shape in outs],
        in_specs=[pl.BlockSpec(memory_space=pltpu.SMEM)]
        + [spec(array.shape, first) for array, first in pairs],
        out_specs=[spec(shape, None if steps == 1 else 0) for shape in outs],
        scratch_shapes=list(scratch),
        compiler_params=pltpu.CompilerParams(vmem_limit_bytes=limit * 1024 * 1024),
        cost_estimate=SHORT,
    )(where, *(array for array, _ in pairs))


def across_kernel(where_ref, own, got, own_high, got_high, *outs):
    low_keep, low_send, high_keep, high_send = outs
    section, side = where_ref[0], where_ref[2]
    rows, half = low_keep.shape[2:]

    def total(first, second, to_side, start, width):
        place = (
            0,
            pl.ds(pl.multiple_of(to_side * rows, 16), rows),
            pl.ds(pl.multiple_of(start, 128), width),
        )
        return add_low(first[place], second[place])

    for to_side in range(2):
        low_keep[0, to_side] = total(own, got, to_side, section * half, half)
        low_send[0, to_side] = total(own, got, to_side, (1 - section) * half, half)
    high_keep[0] = total(own_high, got_high, side, 0, 2 * half)
    high_send[0] = total(own_high, got_high, 1 - side, 0, 2 * half)


def along_kernel(
    where_ref, low, high, low_got, high_got, low_keep, low_send, high_keep, high_send
):
    section, side = where_ref[0], where_ref[2]
    half = low_keep.shape[2]
    for to_side, target in ((side, low_keep), (1 - side, low_send)):
        target[0] = add_low(low[0, to_side], low_got[0, to_side])
    for to_section, target in ((section, high_keep), (1 - section, high_send)):
        columns = pl.ds(pl.multiple_of(to_section * half, 128), half)
        target[0] = add_low(high[0, :, columns], high_got[0, :, columns])


def shards_kernel(where_ref, low, high, low_got, high_got, own, *rest):
    sends, both = rest[:3], rest[3]
    here = where_ref[3]
    for shard in range(2):
        both[shard] = add_low(low[shard], low_got[shard])
        both[2 + shard] = add_low(high[shard], high_got[shard])
    own[...] = both[here]
    for i, target in enumerate(sends):
        target[...] = both[lax.rem(here + 3 - i, 4)]


def pairs_kernel(where_ref, low, high, low_got, high_got, keep, send):
    def put(own, other):
        own[...] = add_low(low[...], low_got[...])
        other[...] = add_low(high[...], high_got[...])

    @pl.when(where_ref[3] < 2)
    def _():
        put(keep, send)

    @pl.when(where_ref[3] >= 2)
    def _():
        put(send, keep)


def single_kernel(where_ref, own, got, keep, send):
    here = lax.rem(where_ref[3], 2)
    keep[...] = add_low(own[here], got[here])
    send[...] = add_low(own[1 - here], got[1 - here])


def back_kernel(counts, where_ref, *refs):
    keep, give = refs[-2:]

    def put(first, second):
        start = position = 0
        for pair in counts:
            width = refs[position].shape[1]
            for count, target in zip(pair, (first, second)):
                terms = refs[position : position + count]
                total = sum(term[...].astype(jnp.float32) for term in terms)
                target[:, start : start + width] = total.astype(jnp.bfloat16)
                position += count
            start += width

    @pl.when(where_ref[0] == 0)
    def _():
        put(keep, give)

    @pl.when(where_ref[0] == 1)
    def _():
        put(give, keep)


def grad_kernel(kinds, where_ref, *refs):
    count = len(kinds)
    lefts, rights = refs[:count], refs[count : 2 * count]
    own, send, sums, total = refs[2 * count :]
    core = where_ref[1]
    step = pl.program_id(0)

    def run(left, right):
        total[...] = contract_rows(left[...], right[...])
        sums[...] = jnp.sum(right[...].astype(jnp.float32), axis=0, keepdims=True)
        parts, rows = own.shape[:2]
        for part in range(parts):
            for to_core, target in ((core, own), (1 - core, send)):
                start = pl.multiple_of((2 * part + to_core) * rows, 32)
                target[part] = total[pl.ds(start, rows), :].astype(jnp.bfloat16)

    first = 0
    for kind, left, right in zip(kinds, lefts, rights):

        @pl.when((step >= first) & (step < first + kind))
        def _(left=left, right=right):
            run(left, right)

        first += kind


def grad_call(where, pairs, deep=False):
    width = 768
    row_count = pairs[0][0].shape[0]
    lefts, rights = [left for left, _ in pairs], [right for _, right in pairs]
    kinds = [max(left.shape[1], right.shape[1]) // width for left, right in pairs]
    steps = sum(kinds)
    firsts = [sum(kinds[:index]) for index in range(len(kinds))]

    def spec(wide, first, kind):
        if not wide:
            return pl.BlockSpec((row_count, width), lambda j: (0, 0))
        return pl.BlockSpec((row_count, width), lambda j: (0, jnp.clip(j - first, 0, kind - 1)))

    in_specs = [pl.BlockSpec(memory_space=pltpu.SMEM)]
    for arrays in (lefts, rights):
        for array, first, kind in zip(arrays, firsts, kinds):
            in_specs.append(spec(array.shape[1] > width, first, kind))
    if deep:
        shape, block = (4, lefts[0].shape[1] // 8, width), (1, lefts[0].shape[1] // 8, width)
        out_spec = pl.BlockSpec(block, lambda j: (j, 0, 0))
        sums_shape, sums_spec = (1, width), pl.BlockSpec((1, width), lambda j: (0, 0))
    else:
        shape, block = (4, width // 8, steps * width), (4, width // 8, width)
        out_spec = pl.BlockSpec(block, lambda j: (0, 0, j))
        sums_shape, sums_spec = (1, steps * width), pl.BlockSpec((1, width), lambda j: (0, j))
    return pl.pallas_call(
        functools.partial(grad_kernel, kinds),
        grid=(steps,),
        out_shape=[jax.ShapeDtypeStruct(shape, jnp.bfloat16)] * 2
        + [jax.ShapeDtypeStruct(sums_shape, jnp.float32)],
        in_specs=in_specs,
        out_specs=[out_spec, out_spec, sums_spec],
        scratch_shapes=[pltpu.VMEM((width, width), jnp.float32)],
        compiler_params=pltpu.CompilerParams(vmem_limit_bytes=16 * 1024 * 1024),
        cost_estimate=SHORT,
    )(where, *lefts, *rights)


GELU_SCALE = 0.7978845608028654
GELU_CUBE = 0.044715


def expand_kernel(normed_ref, weight_ref, bias_ref, active_ref, slope_ref):
    values = jnp.dot(normed_ref[...], weight_ref[...], preferred_element_type=jnp.float32)
    values = values + bias_ref[...]
    square = values * values
    bent = jnp.tanh(GELU_SCALE * values * (1.0 + GELU_CUBE * square))
    half = 0.5 * (1.0 + bent)
    active_ref[...] = (values * half).astype(jnp.bfloat16)
    inner = GELU_SCALE * (1.0 + 3.0 * GELU_CUBE * square)
    slope_ref[...] = (half + 0.5 * values * (1.0 - bent * bent) * inner).astype(jnp.bfloat16)


def expand_call(normed, weight, bias):
    row_count, depth = normed.shape
    columns = weight.shape[1]
    width = depth
    out_spec = pl.BlockSpec((row_count, width), lambda j: (0, j))
    return pl.pallas_call(
        expand_kernel,
        grid=(columns // width,),
        out_shape=[jax.ShapeDtypeStruct((row_count, columns), jnp.bfloat16)] * 2,
        in_specs=[
            pl.BlockSpec((row_count, depth), lambda j: (0, 0)),
            pl.BlockSpec((depth, width), lambda j: (0, j)),
            pl.BlockSpec((1, width), lambda j: (0, j)),
        ],
        out_specs=[out_spec, out_spec],
        compiler_params=pltpu.CompilerParams(vmem_limit_bytes=24 * 1024 * 1024),
        cost_estimate=SHORT,
    )(normed, weight, bias[None])


def slope_kernel(low_ref, weight_ref, slope_ref, out_ref):
    product = times_transpose(low_ref[...], weight_ref[...])
    out_ref[...] = (product * slope_ref[...].astype(jnp.float32)).astype(jnp.bfloat16)


def slope_call(low, weight, slope):
    row_count, width = low.shape
    columns = slope.shape[1]
    block = pl.BlockSpec((row_count, width), lambda j: (0, j))
    return pl.pallas_call(
        slope_kernel,
        grid=(columns // width,),
        out_shape=jax.ShapeDtypeStruct((row_count, columns), jnp.bfloat16),
        in_specs=[
            pl.BlockSpec((row_count, width), lambda j: (0, 0)),
            pl.BlockSpec((width, width), lambda j: (j, 0)),
            block,
        ],
        out_specs=block,
        compiler_params=pltpu.CompilerParams(vmem_limit_bytes=20 * 1024 * 1024),
        cost_estimate=SHORT,
    )(low, weight, slope)


def ordered(own, other, index, axis):
    first = jnp.where(index == 0, own, other)
    second = jnp.where(index == 0, other, own)
    return jnp.concatenate([first, second], axis=axis)


def far_kernel(where_ref, over_x, over_y, low, high):
    low[...] = over_x[...]
    high[...] = over_y[...]


class Moves:
    def __init__(self, where):
        self.where = where

    over_x = staticmethod(lambda array: swap(array, "section", 1))
    over_y = staticmethod(lambda array: swap(array, "replica", 2))
    to_mate = staticmethod(lambda array: swap(array, "replica", 1))

    def gather(self):
        def along(own):
            return ((), [(own, lambda array: lax.all_gather(array, "shard", axis=0))])

        along.late = 1

        def across(chunks):
            return ((chunks,), [(chunks, self.over_x), (chunks, self.over_y)])

        def beyond(*arrays):
            _, over_x, over_y = arrays
            shape = (2, *over_x.shape[1:])
            low, high = local_call(
                far_kernel, self.where, ((over_x, 0), (over_y, 2)), (shape, shape), steps=2
            )
            return (arrays, [(low, self.over_y), (high, self.over_x)])

        return [along, across, beyond]

    def laid(self, state, widths=None):
        theirs = tuple(self.to_mate(piece) for piece in state)
        return place((*state, *theirs), self.where, widths)

    def reduce(self, direct):
        def mates(own, send):
            return ((own,), [(send, self.to_mate)])

        def across(own, got):
            shards, rows, columns = own.shape
            low = (2, 2, rows // 2, columns // 2)
            high = (2, rows // 2, columns)
            result = local_call(
                across_kernel,
                self.where,
                ((own, 0), (got, 0), (own, 2), (got, 2)),
                (low, low, high, high),
                steps=2,
            )
            low_keep, low_send, high_keep, high_send = result
            return ((low_keep, high_keep), [(low_send, self.over_x), (high_send, self.over_y)])

        def along(*state):
            shape = (2, *state[0].shape[2:])
            result = local_call(
                along_kernel, self.where, [(array, 0) for array in state], (shape,) * 4, steps=2
            )
            low_keep, low_send, high_keep, high_send = result
            return ((low_keep, high_keep), [(low_send, self.over_y), (high_send, self.over_x)])

        def shards(*state):
            shape = state[0].shape[1:]
            scratch = [pltpu.VMEM((4, *shape), jnp.bfloat16)]
            result = local_call(shards_kernel, self.where, state, (shape,) * 4, scratch)
            turns = [functools.partial(turn, axis="shard", step=i) for i in (1, 2, 3)]
            return ((result[0],), list(zip(result[1:], turns)))

        def pairs(*state):
            shape = state[0].shape
            keep, send = local_call(pairs_kernel, self.where, state, (shape, shape))
            return ((keep,), [(send, lambda array: swap(array, "shard", 2))])

        def single(own, got):
            shape = own.shape[1:]
            keep, send = local_call(single_kernel, self.where, (own, got), (shape, shape))
            return ((keep,), [(send, lambda array: swap(array, "shard", 1))])

        return [mates, across, along] + ([shards] if direct else [pairs, single])

    def spread(self):
        def back(*pairs):
            terms = [term for pair in pairs for state in pair for term in state]
            rows = terms[0].shape[0]
            shape = (rows, sum(pair[0][0].shape[1] for pair in pairs))
            counts = [tuple(len(state) for state in pair) for pair in pairs]
            kernel = functools.partial(back_kernel, counts)
            keep, give = local_call(kernel, self.where, terms, (shape, shape))
            return ((keep,), [(give, self.over_x)])

        def around(keep, got):
            rows = jnp.stack([keep, got])

            def corner(array):
                over_y = self.over_y(array)
                return (over_y, self.to_mate(over_y))

            return ((rows,), [(rows, self.to_mate), (rows, corner)])

        return [back, around]

    @staticmethod
    def exchange(late):
        def step(section, first, second):
            give = jnp.where(section == 0, second, first)
            if not late:
                return ((), [(give, Moves.over_x)])
            return ((), [(give, lambda array: lax.all_gather(array, "section", axis=0))])

        step.late = late
        return [step]

    def total(self):
        def chip(array):
            return ((array,), [(array, self.to_mate)])

        def step_of(move):
            def step(own, got):
                array = own + got
                return ((array,), [(array, move)])

            return step

        moves = (self.over_x, self.over_y, lambda a: swap(a, "shard", 2), lambda a: swap(a, "shard", 1))
        return [chip] + [step_of(move) for move in moves]


class Flows:
    def __init__(self):
        self.left = {}
        self.states = {}
        self.open = {}

    def start(self, name, steps, *state):
        self.left[name] = list(steps)
        self.states[name] = state

    def extend(self, name, steps):
        self.left[name] += steps

    def stage(self, compute=lambda: (), *inputs):
        names = [name for name in self.left if self.left[name]]
        steps = {name: self.left[name].pop(0) for name in names}
        names = [name for name in names if steps[name] is not None]
        steps = [steps[name] for name in names]
        states = [self.states[name] for name in names]
        inputs, states = lax.optimization_barrier((inputs, states))
        ready = [step(*state) for step, state in zip(steps, states)]
        kept = [keep for keep, _ in ready]
        sent = [[array for array, _ in sends] for _, sends in ready]
        got = [
            [move(array) for array, (_, move) in zip(arrays, sends)]
            for arrays, (_, sends) in zip(sent, ready)
        ]
        late = [getattr(step, "late", 0) for step in steps]
        waited = [result for result, slow in zip(got, late) if not slow]
        due = [name for name in self.open if self.open[name] == 1]
        closing = [self.states[name] for name in due]
        results, waited, closing = lax.optimization_barrier((compute(*inputs), waited, closing))
        self.states.update(zip(due, closing))
        self.open = {name: left - 1 for name, left in self.open.items() if left > 1}
        self.open.update({name: slow for name, slow in zip(names, late) if slow})
        waited = iter(waited)
        for name, keep, result, slow in zip(names, kept, got, late):
            self.states[name] = (*keep, *(result if slow else next(waited)))
        return results


def close_kernel(where_ref, *refs):
    section, core, side = (where_ref[i] for i in range(3))
    wide_pieces, last_pieces = refs[:4], refs[4:8]
    input_out, expand_out, output_out, contract_out = refs[8:]
    input_half = input_out.shape[1] // 2
    contract_half = contract_out.shape[1] // 2
    split = expand_out.shape[1] - (wide_pieces[0].shape[2] - input_half)

    def one(far_core, far_side, far_section):
        at_section = section if far_section == 0 else 1 - section
        at_side = side if far_side == 0 else 1 - side
        at_core = core if far_core == 0 else 1 - core
        rank = at_core * 2 + at_side
        wide = wide_pieces[far_core * 2 + far_side][far_section].astype(jnp.float32)
        rows = pl.ds(pl.multiple_of(rank * wide.shape[0], 16), wide.shape[0])
        columns = pl.ds(pl.multiple_of(at_section * input_half, 128), input_half)
        input_out[rows, columns] = wide[:, :input_half]
        wide = wide[:, input_half:]

        @pl.when(at_section == 0)
        def _():
            expand_out[rows, : wide.shape[1]] = wide

        @pl.when(at_section == 1)
        def _():
            expand_out[rows, wide.shape[1] :] = wide[:, :split]
            output_out[rows, :] = wide[:, split:]

        last = last_pieces[far_core * 2 + far_side][far_section].astype(jnp.float32)
        rows = pl.ds(pl.multiple_of(rank * last.shape[0], 16), last.shape[0])
        columns = pl.ds(pl.multiple_of(at_section * contract_half, 128), contract_half)
        contract_out[rows, columns] = last

    for far_core in range(2):
        for far_side in range(2):
            for far_section in range(2):
                one(far_core, far_side, far_section)


def close(where, wide, contract, shapes):
    def pieces(state):
        own, mate, (over_y, mate_y) = state
        return (own, over_y, mate, mate_y)

    arrays = (*pieces(wide), *pieces(contract))
    return local_call(close_kernel, where, arrays, shapes, kind=jnp.float32, limit=32)

VECTORS = ("gain_a", "shift_a", "bias_q", "bias_v", "bias_o", "gain_f", "shift_f", "bias_c")


def forward_attention(params, hidden_low, segment):
    hidden = hidden_low.astype(jnp.float32)
    normed, stats_a = layer_norm(hidden, params["gain_a"], params["shift_a"])
    normed = normed.astype(jnp.bfloat16)
    zeros = jnp.zeros_like(params["bias_q"])
    joint_bias = jnp.concatenate([params["bias_q"], zeros, params["bias_v"]])
    joint_low = (
        jnp.dot(normed, params["input"], preferred_element_type=jnp.float32) + joint_bias
    ).astype(jnp.bfloat16)
    mixed_low, log_sums = attend_forward(joint_low, segment)
    middle = (
        hidden
        + jnp.dot(mixed_low, params["output"], preferred_element_type=jnp.float32)
        + params["bias_o"]
    )
    return dict(
        hidden_low=hidden_low,
        normed=normed,
        stats_a=stats_a,
        joint_low=joint_low,
        log_sums=log_sums,
        mixed_low=mixed_low,
        middle=middle,
    )


def forward_expand(params, middle):
    normed_two, stats_f = layer_norm(middle, params["gain_f"], params["shift_f"])
    normed_two = normed_two.astype(jnp.bfloat16)
    activated, slope = expand_call(normed_two, params["expand"], params["bias_e"])
    return dict(normed_two=normed_two, stats_f=stats_f, slope=slope, activated=activated)


def forward_contract(params, middle, activated, living):
    result = (
        middle
        + jnp.dot(activated, params["contract"], preferred_element_type=jnp.float32)
        + params["bias_c"]
    )
    return (result * living[:, None]).astype(jnp.bfloat16)


class Backward:
    def __init__(self, params, kept, segment, living, where, upstream):
        self.params, self.segment, self.living, self.where = params, segment, living, where
        self.held = dict(kept, upstream=upstream)

    def run(self, flow, part):
        function, names = {
            "expand": (self.expand, ("upstream", "activated", "slope")),
            "norm": (
                self.norm,
                ("expand_low", "normed_two", "out_grad", "middle", "stats_f", "mixed_low"),
            ),
            "attention": (self.attention, ("joint_low", "log_sums", "mixed_grad")),
            "input": (self.input, ("normed", "joint_grad")),
            "last": (self.last, ("joint_grad", "middle_grad", "hidden_low", "stats_a")),
            "both": (
                self.both,
                ("normed", "joint_grad", "middle_grad", "hidden_low", "stats_a"),
            ),
        }[part]
        self.held.update(flow.stage(function, *(self.held[name] for name in names)))

    def grads(self, name, *pairs, deep=False):
        if self.where is not None:
            own, send, sums = grad_call(self.where, pairs, deep)
            return {name + "_own": own, name + "_send": send, name + "_sums": sums[0]}
        whole = jnp.concatenate([contract_rows(*pair).astype(jnp.bfloat16) for pair in pairs], axis=1)
        sums = [jnp.sum(right.astype(jnp.float32), axis=0) for _, right in pairs]
        return {name + "_own": whole, name + "_sums": jnp.concatenate(sums)}

    def expand(self, upstream, activated, slope):
        out_grad = upstream.astype(jnp.float32) * self.living[:, None]
        low = out_grad.astype(jnp.bfloat16)
        found = self.grads("contract", (activated, low), deep=True)
        expand_low = slope_call(low, self.params["contract"], slope)
        return dict(found, out_grad=out_grad, expand_low=expand_low)

    def norm(self, expand_low, normed_two, out_grad, middle, stats_f, mixed_low):
        normed_grad = times_transpose(expand_low, self.params["expand"])
        norm_grad, gain_grad, shift_grad = layer_norm_back(
            middle, stats_f, self.params["gain_f"], normed_grad
        )
        middle_grad = out_grad + norm_grad
        branch_low = middle_grad.astype(jnp.bfloat16)
        mixed_grad = times_transpose(branch_low, self.params["output"]).astype(jnp.bfloat16)
        found = self.grads("expand", (normed_two, expand_low), (mixed_low, branch_low))
        return dict(
            found, middle_grad=middle_grad, mixed_grad=mixed_grad, gain_f=gain_grad, shift_f=shift_grad
        )

    def attention(self, joint_low, log_sums, mixed_grad):
        return dict(joint_grad=attend_backward(joint_low, log_sums, mixed_grad, self.segment))

    def input(self, normed, joint_grad):
        return self.grads("input", (normed, joint_grad))

    def last(self, joint_grad, middle_grad, hidden_low, stats_a):
        normed_grad = times_transpose(joint_grad, self.params["input"])
        norm_grad, gain_grad, shift_grad = layer_norm_back(
            hidden_low.astype(jnp.float32), stats_a, self.params["gain_a"], normed_grad
        )
        grad = middle_grad + norm_grad
        return dict(grad_low=grad.astype(jnp.bfloat16), gain_a=gain_grad, shift_a=shift_grad)

    def both(self, normed, joint_grad, middle_grad, hidden_low, stats_a):
        found = self.input(normed, joint_grad)
        return dict(found, **self.last(joint_grad, middle_grad, hidden_low, stats_a))

    def small(self):
        held = self.held
        width = held["gain_a"].shape[0]
        split = held["expand_sums"].shape[0] - width
        held = dict(
            held,
            bias_q=held["input_sums"][:width],
            bias_v=held["input_sums"][2 * width :],
            bias_o=held["expand_sums"][split:],
            bias_c=held["contract_sums"],
        )
        vectors = [held[name] for name in VECTORS] + [held["expand_sums"][:split]]
        return jnp.concatenate(vectors).reshape(-1, width)


def per_device(
    tokens,
    cotangent,
    lengths,
    assignment,
    attention_gain,
    attention_shift,
    input_weight,
    query_bias,
    value_bias,
    output_weight,
    output_bias,
    feedforward_gain,
    feedforward_shift,
    expand_weight,
    expand_bias,
    contract_weight,
    contract_bias,
):
    section = lax.axis_index("section")
    shard = lax.axis_index("shard")
    replica = lax.axis_index("replica")
    shards, replicas = lax.axis_size("shard"), lax.axis_size("replica")
    core, side = replica % 2, replica // 2
    model_width = tokens.shape[1]
    cube = shards == 4 and replicas == 4
    where = jnp.stack([section, core, side, shard]).astype(jnp.int32)

    slot = (shard * replicas + replica) * MICRO + section
    matches = (assignment == slot).astype(jnp.int32)
    counts = jnp.sum(matches[:, None] * lengths, axis=0, dtype=jnp.int32)
    segment, living = slot_layout(counts, ROWS)
    entering = lax.dynamic_slice_in_dim(tokens, section * ROWS, ROWS, 0)
    seed = lax.dynamic_slice_in_dim(cotangent, section * ROWS, ROWS, 0)

    vectors = (
        attention_gain,
        attention_shift,
        query_bias,
        value_bias,
        output_bias,
        feedforward_gain,
        feedforward_shift,
        contract_bias,
        expand_bias,
    )
    small_own = jnp.concatenate(vectors, axis=1)
    expand_width = expand_weight.shape[2]
    flow = Flows()
    moves = Moves(where)

    def joined(members):
        return [member.reshape(-1, member.shape[-1]) for member in members]

    def named(small_all, **pairs):
        count = len(VECTORS)
        split = small_all.shape[2] - expand_bias.shape[1]
        lines = small_all[:, :, :split].reshape(2, shards, count, split // count)
        lines = lines.transpose(0, 2, 1, 3).reshape(2, count, model_width).astype(jnp.float32)
        bias_e = small_all[:, :, split:].reshape(2, expand_width).astype(jnp.float32)
        found = []
        for block in range(2):
            params = {name: lines[block, index] for index, name in enumerate(VECTORS)}
            params["bias_e"] = bias_e[block]
            params.update({name: pair[block] for name, pair in pairs.items()})
            found.append(params)
        return found

    if cube:

        def chunk(weight):
            size = weight.shape[1] // 4
            return lax.dynamic_slice_in_dim(weight[0], (core * 2 + side) * size, size, 0)

        input_chunk, output_chunk = chunk(input_weight), chunk(output_weight)
        small_rows = small_own.shape[1] // 128
        short = input_chunk.shape[0] - small_rows
        padded = jnp.pad(small_own.reshape(small_rows, 128), ((0, short), (0, 0)))
        opening = jnp.concatenate([input_chunk, output_chunk, padded], axis=1)
        widths = (input_chunk.shape[1], output_chunk.shape[1], 128)
        flow.start("gather_open", moves.gather(), opening)
        flow.stage()
        flow.start("gather_expand", moves.gather(), chunk(expand_weight))
        flow.stage()
        flow.start("gather_contract", moves.gather(), chunk(contract_weight))
        flow.stage()

        def open_part(state, hidden_low):
            laid = moves.laid(state, widths)
            small_all = jnp.stack(laid[2::3])[:, :, 0, :small_rows].reshape(2, shards, -1)
            found = named(small_all, input=joined(laid[0::3]), output=joined(laid[1::3]))
            return (found, forward_attention(found[0], hidden_low, segment))

        (params, kept_first) = flow.stage(open_part, flow.states["gather_open"], entering)

        def middle_part(state, middle):
            expand_all = joined(moves.laid(state))
            held = forward_expand(dict(params[0], expand=expand_all[0]), middle)
            return (expand_all, held)

        expand_all, held = flow.stage(
            middle_part, flow.states["gather_expand"], kept_first["middle"]
        )
        kept_first.update(held)
        contract_all = joined(moves.laid(flow.states["gather_contract"]))
        for block in range(2):
            params[block].update(expand=expand_all[block], contract=contract_all[block])
    else:

        def whole(weight):
            held = lax.all_gather(weight, "shard", axis=1, tiled=True)
            return lax.all_gather(held, "section", axis=0, tiled=True)

        params = named(
            whole(small_own[None]),
            input=whole(input_weight),
            output=whole(output_weight),
            expand=whole(expand_weight),
            contract=whole(contract_weight),
        )
        kept_first = forward_attention(params[0], entering, segment)
        kept_first.update(forward_expand(params[0], kept_first["middle"]))

    middle_out = forward_contract(
        params[0], kept_first["middle"], kept_first["activated"], living
    )

    def second_forward(hidden_low):
        kept = forward_attention(params[1], hidden_low, segment)
        kept.update(forward_expand(params[1], kept["middle"]))
        return (kept, forward_contract(params[1], kept["middle"], kept["activated"], living))

    kept_second, last_out = second_forward(middle_out)

    def begin(block, name, direct=False):
        tag = ("first_" if block is first else "second_") + name
        if cube:
            flow.start(tag, moves.reduce(direct), block.held[name + "_own"], block.held[name + "_send"])

    def spread(name, *members):
        if cube:
            pairs = [(flow.states["first_" + m], flow.states["second_" + m]) for m in members]
            back, around = moves.spread()
            steps = [back, around] if name == "wide" else [back, None, around]
            flow.start(name, steps, *pairs)

    first = None
    second = Backward(params[1], kept_second, segment, living, where if cube else None, seed)
    flow.start("out", moves.exchange(0), section, middle_out, last_out)
    second.run(flow, "expand")
    begin(second, "contract")
    second.run(flow, "norm")
    begin(second, "expand")
    second.run(flow, "attention")
    second.run(flow, "both")
    begin(second, "input")

    first = Backward(params[0], kept_first, segment, living, where if cube else None, second.held["grad_low"])
    first.run(flow, "expand")
    begin(first, "contract")
    first.run(flow, "norm")
    begin(first, "expand")
    first.run(flow, "attention")
    first.run(flow, "input")
    begin(first, "input", direct=True)
    first.run(flow, "last")
    small_both = jnp.stack([first.small(), second.small()])
    flow.start("small", moves.total() if cube else [], small_both)
    flow.start("grad", moves.exchange(4), section, first.held["grad_low"], second.held["grad_low"])
    flow.stage()
    spread("contract", "contract")
    flow.stage()
    flow.stage()
    spread("wide", "input", "expand")
    flow.stage()
    flow.stage()

    def own_block(name, first_value, second_value):
        keep = jnp.where(section == 0, first_value, second_value)
        got = flow.states[name][0]
        got = pick(got, 1 - section, 0) if got.ndim == 3 else got
        return ordered(keep, got, section, 0)

    block_out = own_block("out", middle_out, last_out)
    grad_out = own_block("grad", first.held["grad_low"], second.held["grad_low"])
    grad_out = grad_out.astype(jnp.float32)

    if cube:
        small_sum = flow.states["small"][0] + flow.states["small"][1]
        shapes = [
            weight.shape[1:] for weight in (input_weight, expand_weight, output_weight, contract_weight)
        ]
        large = close(where, flow.states["wide"], flow.states["contract"], shapes)
    else:
        small_sum = lax.psum(small_both, ("section", "shard", "replica"))
        large = []
        for name in ("input_own", "expand_own", "contract_own"):
            wide = jnp.stack([block.held[name] for block in (first, second)])
            held = lax.psum_scatter(wide, "section", scatter_dimension=0, tiled=True)
            held = lax.psum_scatter(held[0], "shard", scatter_dimension=0, tiled=True)
            large.append(lax.psum(held, "replica").astype(jnp.float32))
        large[1:2] = [large[1][:, :expand_width], large[1][:, expand_width:]]
    small_sum = pick(small_sum, section, 0)
    lines = small_sum[: len(VECTORS)].reshape(len(VECTORS), shards, -1)
    lines = pick(lines, shard, 1)
    small = {name: lines[index][None] for index, name in enumerate(VECTORS)}
    bias_e_grad = pick(small_sum[len(VECTORS) :].reshape(shards, -1), shard, 0)[None]
    input_grad, expand_grad, output_grad, contract_grad = (member[None] for member in large)
    return (
        block_out[None],
        grad_out[None],
        small["gain_a"],
        small["shift_a"],
        input_grad,
        small["bias_q"],
        small["bias_v"],
        output_grad,
        small["bias_o"],
        small["gain_f"],
        small["shift_f"],
        expand_grad,
        bias_e_grad,
        contract_grad,
        small["bias_c"],
    )


def solution(mesh):
    placed = (
        P(("shard", "replica"), None),
        P(("shard", "replica"), None),
        P(),
        P(),
        P("section", "shard"),
        P("section", "shard"),
        P("section", "shard", None),
        P("section", "shard"),
        P("section", "shard"),
        P("section", "shard", None),
        P("section", "shard"),
        P("section", "shard"),
        P("section", "shard"),
        P("section", "shard", None),
        P("section", "shard"),
        P("section", "shard", None),
        P("section", "shard"),
    )
    return jax.shard_map(
        per_device,
        mesh=mesh,
        in_specs=placed,
        out_specs=(
            P("section", ("shard", "replica"), None),
            P("section", ("shard", "replica"), None),
            P("section", "shard"),
            P("section", "shard"),
            P("section", "shard", None),
            P("section", "shard"),
            P("section", "shard"),
            P("section", "shard", None),
            P("section", "shard"),
            P("section", "shard"),
            P("section", "shard"),
            P("section", "shard", None),
            P("section", "shard"),
            P("section", "shard", None),
            P("section", "shard"),
        ),
        check_vma=False,
    )
```
